256 devices in a mesh: gx: 64 (over z, y, core), gy: 4 (over x).
Axes of the slice: x: 4, y: 4, z: 8, core: 2. Of those that a mesh axis runs over, the one named last changes fastest.
Arguments:
- pressure: float32 [1024, 256, 128], P('gx', 'gy'), may hold values from -6 to 6
- inverse_density: float32 [1024, 256, 128], P('gx', 'gy'), may hold values from 0.04 to 2
- source: float32 [1024, 256, 128], P('gx', 'gy'), may hold values from -6 to 6
Outputs:
- updated_pressure: float32 [1024, 256, 128], P('gx', 'gy')
- residual: float32 [1024, 256, 128], P('gx', 'gy')
The draws below stay inside these ranges and needn't reach their ends.
All inputs are finite; a program needn't handle non-finite values.
Results may differ from the reference program's by a relative error of at most 0.0003.
Values sent between devices are 32-bit elements; how exact they have to be, the bound alone decides.
A program may use at most 192 MiB of HBM per device.

```python
import math
import jax
import jax.numpy as jnp

NZ = 128
LEVELS = 4
PRE = 2
POST = 2
COARSE = 8
NX = 1024
NY = 256


def region_offset(key):
    return jax.random.randint(key, (), 0, NX // 2 ** LEVELS)


def draw_inverse_density(key, part):
    offset_cells = region_offset(key)
    key = jax.random.fold_in(key, 11)
    block_size = 2 ** LEVELS
    cells_x = NX // block_size
    grid_shape = (NX, NY, NZ)
    x_cells = (jnp.arange(NX, dtype=jnp.int32) // block_size)[:, None, None]
    y_cells = (jnp.arange(NY, dtype=jnp.int32) // block_size)[None, :, None]
    z_cells = (jnp.arange(NZ, dtype=jnp.int32) // block_size)[None, None, :]
    first_half = (x_cells - offset_cells) % cells_x < cells_x // 2
    along_x = (y_cells + z_cells) % 2 == 0
    along_y = (x_cells + z_cells) % 2 == 0
    high_cells = jnp.where(first_half, along_x, along_y)
    base_level = jnp.where(high_cells, jnp.float32(1.0), jnp.float32(0.04))
    rough_part = jnp.exp(jax.random.uniform(key, grid_shape, jnp.float32, 0.0, math.log(2.0)))
    return (base_level * rough_part).astype(jnp.float32)


def draw_source(key, part):
    offset_cells = region_offset(key)
    key = jax.random.fold_in(key, 23)
    block_size = 2 ** LEVELS
    grid_shape = (NX, NY, NZ)
    x_coords = jnp.arange(NX, dtype=jnp.float32) + 0.5
    centre = offset_cells.astype(jnp.float32) * block_size + NX / 4.0
    wave_part = jnp.cos(2.0 * math.pi * (x_coords - centre) / NX)[:, None, None]
    rough_part = jax.random.normal(key, grid_shape, jnp.float32)
    smooth = 0.02 * wave_part
    return jnp.clip(rough_part + smooth, -6.0, 6.0).astype(jnp.float32)


def level_of(rng, extent, pieces, low, high):
    def one(position, blocks):
        draws = jax.random.uniform(jax.random.fold_in(jax.random.fold_in(rng, 6), position), (blocks,), jnp.float32, low / len(pieces), high / len(pieces))
        return jnp.repeat(jnp.exp(draws), extent[position] // blocks).reshape((-1,) + (1,) * (len(extent) - position - 1))

    level = one(*pieces[0])
    for cut in pieces[1:]:
        level = level * one(*cut)
    return level


def normal_values(stream_key, shape, width, most, pieces=(), kind=jnp.bfloat16):
    array = jax.random.normal(stream_key, shape, jnp.float32) * width
    if len(pieces) > 0:
        array = level_of(stream_key, shape, pieces, -0.22, 0.18) * array
    return jnp.clip(array, min=-most, max=most).astype(kind)


def setup_inputs(seed: int = 0) -> dict:
    key_list = jax.random.split(jax.random.key(seed), 4)
    pressure = normal_values(key_list[0], (NX, NY, NZ), 1.0, 6.0, ((0, 64), (1, 4)), jnp.float32)
    inverse_density = draw_inverse_density(jax.random.fold_in(key_list[3], 71), 0)
    source = draw_source(jax.random.fold_in(key_list[3], 71), 0)
    return {"pressure": pressure, "inverse_density": inverse_density, "source": source}


OMEGA = 0.8


def neighbor_terms(padded_press, padded_coef, factor):
    centre = padded_press[1:-1, 1:-1]
    centre_k = padded_coef[1:-1, 1:-1]
    neighbours = [
        (padded_press[2:, 1:-1], padded_coef[2:, 1:-1]),
        (padded_press[:-2, 1:-1], padded_coef[:-2, 1:-1]),
        (padded_press[1:-1, 2:], padded_coef[1:-1, 2:]),
        (padded_press[1:-1, :-2], padded_coef[1:-1, :-2]),
        (jnp.roll(centre, -1, 2), jnp.roll(centre_k, -1, 2)),
        (jnp.roll(centre, 1, 2), jnp.roll(centre_k, 1, 2)),
    ]
    fluxes = jnp.zeros_like(centre)
    totals = jnp.zeros_like(centre)
    for near_press, near_coef in neighbours:
        face_coef = 2.0 * centre_k * near_coef / (centre_k + near_coef)
        totals = totals + face_coef
        fluxes = fluxes + face_coef * (centre - near_press)
    return factor * fluxes, factor * totals


def relax(padded_press, padded_coef, source_part, factor):
    applied, diagonal = neighbor_terms(padded_press, padded_coef, factor)
    return padded_press[1:-1, 1:-1] + OMEGA * (source_part - applied) / diagonal


def coarsen(field):
    sx, sy, sz = field.shape
    return field.reshape(sx // 2, 2, sy // 2, 2, sz // 2, 2).mean(axis=(1, 3, 5))


def refine(field):
    return jnp.repeat(jnp.repeat(jnp.repeat(field, 2, 0), 2, 1), 2, 2)


def wrapped(field):
    return jnp.pad(field, ((1, 1), (1, 1), (0, 0)), mode="wrap")


def reference(pressure, inverse_density, source):
    coefficients = [inverse_density]
    for level_index in range(LEVELS):
        coefficients.append(coarsen(coefficients[-1]))
    current = pressure
    target = source
    saved_levels = []
    for level_index in range(LEVELS):
        factor = 0.25 ** level_index
        padded_coef = wrapped(coefficients[level_index])
        for sweep_index in range(PRE):
            current = relax(wrapped(current), padded_coef, target, factor)
        applied, unused = neighbor_terms(wrapped(current), padded_coef, factor)
        saved_levels.append((current, target))
        target = coarsen(target - applied)
        current = jnp.zeros_like(target)
    factor = 0.25 ** LEVELS
    padded_coef = wrapped(coefficients[LEVELS])
    for sweep_index in range(COARSE):
        current = relax(wrapped(current), padded_coef, target, factor)
    for level_index in reversed(range(LEVELS)):
        factor = 0.25 ** level_index
        padded_coef = wrapped(coefficients[level_index])
        below, target = saved_levels[level_index]
        current = below + refine(current)
        for sweep_index in range(POST):
            current = relax(wrapped(current), padded_coef, target, factor)
    applied, unused = neighbor_terms(wrapped(current), wrapped(inverse_density), 1.0)
    return current, source - applied
```

```python
import functools

import jax
import jax.numpy as jnp
from jax import lax
from jax.experimental import pallas as pl
from jax.experimental.pallas import tpu as pltpu
from jax.sharding import PartitionSpec as P

MESH = pl.DeviceIdType.MESH
F32 = jnp.float32
OMEGA = 0.8
LANES = 128
SIDES = ((-1, 0), (1, 0), (0, -1), (0, 1), (-1, -1), (-1, 1), (1, -1), (1, 1))
REACH_G = 10
REACH_K = 11
SLOTS = 24
PEERS_K = [o for d in range(REACH_K, 0, -1) for o in (d, -d)]
PEERS_G = [o for d in range(REACH_G, 0, -1) for o in (d, -d)]


def recip(x):
    y = pl.reciprocal(x, approx=True)
    return y * (2.0 - x * y)


def roll(x, shift, axis):
    return pltpu.roll(x, shift % x.shape[axis], axis)


def loop(lo, hi, body):
    def step(i, carry):
        body(i)
        return carry

    lax.fori_loop(lo, hi, step, 0)


def strips(lo, hi, size=16):
    return [(r, min(size, hi - r)) for r in range(lo, hi, size)]


def lane_index(shape):
    return lax.broadcasted_iota(jnp.int32, shape, 1)


def pair_sum_z(x, s):
    first = (lane_index(x.shape) // s) % 2 == 0
    return x + jnp.where(first, roll(x, -s, 1), roll(x, s, 1))


class Level:
    def __init__(self, s, scale, k, r, fx, fy, fz, w, d):
        self.s, self.scale, self.k = s, scale, k
        self.r, self.fx, self.fy, self.fz, self.w, self.d = r, fx, fy, fz, w, d

    def inverses(self, planes, rows):
        def body(x):
            for r, n in rows:
                self.r[x, pl.ds(r, n), :] = (0.5 / self.scale) * recip(self.k[x, pl.ds(r, n), :])

        loop(*planes, body)

    def faces(self, planes, rows):
        def body(x):
            for r, n in rows:
                here = self.r[x, pl.ds(r, n), :]
                self.fx[x, pl.ds(r, n), :] = recip(here + self.r[x + 1, pl.ds(r, n), :])
                self.fy[x, pl.ds(r, n), :] = recip(here + self.r[x, pl.ds(r + 1, n), :])
                self.fz[x, pl.ds(r, n), :] = recip(here + roll(here, -self.s, 1))

        loop(*planes, body)

    def diagonal(self, planes, rows):
        def body(x):
            for r, n in rows:
                fz = self.fz[x, pl.ds(r, n), :]
                d = self.fx[x, pl.ds(r, n), :] + self.fx[x - 1, pl.ds(r, n), :]
                d += self.fy[x, pl.ds(r, n), :] + self.fy[x, pl.ds(r - 1, n), :]
                d += fz + roll(fz, self.s, 1)
                self.d[x, pl.ds(r, n), :] = d
                self.w[x, pl.ds(r, n), :] = OMEGA * recip(d)

        loop(*planes, body)

    def around(self, v, x, r, n):
        here = v[x, pl.ds(r, n), :]
        fz = self.fz[x, pl.ds(r, n), :]
        a = self.fx[x, pl.ds(r, n), :] * v[x + 1, pl.ds(r, n), :]
        a += self.fx[x - 1, pl.ds(r, n), :] * v[x - 1, pl.ds(r, n), :]
        a += self.fy[x, pl.ds(r, n), :] * v[x, pl.ds(r + 1, n), :]
        a += self.fy[x, pl.ds(r - 1, n), :] * v[x, pl.ds(r - 1, n), :]
        a += fz * roll(here, -self.s, 1) + roll(fz * here, self.s, 1)
        return here, a

    def first_sweep(self, g, dst, planes, rows):
        def body(x):
            for r, n in rows:
                dst[x, pl.ds(r, n), :] = self.w[x, pl.ds(r, n), :] * g[x, pl.ds(r, n), :]

        loop(*planes, body)

    def sweep(self, src, g, dst, planes, rows):
        def body(x):
            for r, n in rows:
                here, a = self.around(src, x, r, n)
                w = self.w[x, pl.ds(r, n), :]
                dst[x, pl.ds(r, n), :] = (1.0 - OMEGA) * here + w * (g[x, pl.ds(r, n), :] + a)

        loop(*planes, body)

    def residual(self, v, g, x, r, n):
        here, a = self.around(v, x, r, n)
        return g[x, pl.ds(r, n), :] + a - self.d[x, pl.ds(r, n), :] * here


def coarsen(value, s, tmp, dst, pairs, rows, dst_rows):
    lo, hi, plane = pairs

    def gather(j):
        x = plane(j)
        for r, n in rows:
            tmp[j, pl.ds(r, n), :] = pair_sum_z(value(x, r, n) + value(x + 1, r, n), s)

    loop(lo, hi, gather)
    first, count = rows[0][0], sum(n for _, n in rows) // 2

    def squeeze(j):
        even = tmp[j, pl.ds(first, count, stride=2), :]
        odd = tmp[j, pl.ds(first + 1, count, stride=2), :]
        dst[j, pl.ds(dst_rows, count), :] = 0.125 * (even + odd)

    loop(lo, hi, squeeze)


class Packed3:
    def __init__(self, shape):
        lane = lane_index(shape)
        self.y_last, self.y_first = lane >= 112, lane < 16
        self.z_last, self.z_first = lane % 16 == 15, lane % 16 == 0

    def y_next(self, v):
        t = [roll(a, -16, 1) for a in v]
        return [jnp.where(self.y_last, t[(i + 2) % 8], t[i]) for i in range(8)]

    def y_prev(self, v):
        t = [roll(a, 16, 1) for a in v]
        return [jnp.where(self.y_first, t[(i - 2) % 8], t[i]) for i in range(8)]

    def z_next(self, v):
        return [jnp.where(self.z_last, roll(a, 15, 1), roll(a, -1, 1)) for a in v]

    def z_prev(self, v):
        return [jnp.where(self.z_first, roll(a, -15, 1), roll(a, 1, 1)) for a in v]

    def x_next(self, v):
        return [v[i + 1] if i % 2 == 0 else roll(v[i - 1], -1, 0) for i in range(8)]

    def x_prev(self, v):
        return [roll(v[i + 1], 1, 0) if i % 2 == 0 else v[i - 1] for i in range(8)]

    def both(self, f, v):
        out = None
        for axis in range(3):
            nxt = (self.x_next, self.y_next, self.z_next)[axis](v)
            prv = (self.x_prev, self.y_prev, self.z_prev)[axis]([a * b for a, b in zip(f[axis], v)])
            term = [a * b + c for a, b, c in zip(f[axis], nxt, prv)]
            out = term if out is None else [a + b for a, b in zip(out, term)]
        return out


class Packed4(Packed3):
    def __init__(self, shape):
        lane = lane_index(shape)
        self.z_last, self.z_first = lane % 8 == 7, lane % 8 == 0

    def y_next(self, v):
        return [roll(v[0], -8, 1)]

    def y_prev(self, v):
        return [roll(v[0], 8, 1)]

    def z_next(self, v):
        return [jnp.where(self.z_last, roll(v[0], 7, 1), roll(v[0], -1, 1))]

    def z_prev(self, v):
        return [jnp.where(self.z_first, roll(v[0], -7, 1), roll(v[0], 1, 1))]

    def x_next(self, v):
        return [roll(v[0], -1, 0)]

    def x_prev(self, v):
        return [roll(v[0], 1, 0)]


def packed_coefs(pack, k, scale):
    r = [(0.5 / scale) * recip(a) for a in k]
    f = []
    d = None
    for nxt, prv in ((pack.x_next, pack.x_prev), (pack.y_next, pack.y_prev), (pack.z_next, pack.z_prev)):
        face = [recip(a + b) for a, b in zip(r, nxt(r))]
        f.append(face)
        both = [a + b for a, b in zip(face, prv(face))]
        d = both if d is None else [a + b for a, b in zip(d, both)]
    return f, d


def packed_sweep(pack, f, w, v, g):
    return [
        (1.0 - OMEGA) * a + b * (c + e) for a, b, c, e in zip(v, w, g, pack.both(f, v))
    ]


def dot(a, b):
    return jnp.dot(a, b, precision=lax.Precision.HIGHEST, preferred_element_type=F32)


def grid2(shape):
    return lax.broadcasted_iota(jnp.int32, shape, 0), lax.broadcasted_iota(jnp.int32, shape, 1)


def pack_rows(cells):
    l, t = grid2((LANES, LANES))
    choose = jnp.where((l // 8 == t % 16) & (l % 4 == 0), 0.125, 0.0).astype(F32)
    r, t = grid2((16, LANES))
    keep = r // 2 == t // 16
    rows = []
    for p in range(2):
        u = dot(cells[2 * p] + cells[2 * p + 1], choose)
        rows.append(jnp.sum(jnp.where(keep, u, 0.0), axis=0, keepdims=True))
    return rows


def kernel(
    ngx, ngy, p_hbm, k_hbm, s_hbm, v_out, r_out,
    w0, r0, fx0, fy0, fz0, wt0, d0, va0, vb0, vs0, res0,
    k1, r1, fx1, fy1, fz1, wt1, d1, g1, va1, vb1, dup1,
    k2, r2, fx2, fy2, fz2, wt2, d2, g2, va2, vb2, w2, dup2,
    tmp1, tmp2, yk, yg, xk, xg, c3, c4, v3,
    load_sem, store_sem, side_s, side_r, y_s, y_r, xk_s, xk_r, xg_s, xg_r,
):
    gx, gy = lax.axis_index("gx"), lax.axis_index("gy")

    def peer(dx, dy):
        return (lax.rem(gx + (dx + ngx), ngx), lax.rem(gy + (dy + ngy), ngy))

    loads = [
        pltpu.make_async_copy(hbm, w0.at[i, pl.ds(3, 16), pl.ds(16, 64), :], load_sem.at[i])
        for i, hbm in ((1, k_hbm), (0, p_hbm), (2, s_hbm))
    ]
    for c in loads:
        c.start()

    greet = list(SIDES) + [(0, 2)] + [(o, 0) for o in PEERS_K if abs(o) > 1]
    barrier = pltpu.get_barrier_semaphore()
    for o in greet:
        pl.semaphore_signal(barrier, inc=1, device_id=peer(*o), device_id_type=MESH)

    waits = []

    def exchange(which, src, dst, x0, nx, hx, ny):
        y0, hy = 16, 8
        lead = (slice(None),) * (len(src.shape) - 3)
        copies = []
        for i, (dx, dy) in enumerate(SIDES):
            xs, xd, xn = ((x0, x0 + nx, hx), (x0, x0, nx), (x0 + nx - hx, x0 - hx, hx))[dx + 1]
            ys, yd, yn = ((y0, y0 + ny, hy), (y0, y0, ny), (y0 + ny - hy, y0 - hy, hy))[dy + 1]
            c = pltpu.make_async_remote_copy(
                src_ref=src.at[lead + (pl.ds(xs, xn), pl.ds(ys, yn))],
                dst_ref=dst.at[lead + (pl.ds(xd, xn), pl.ds(yd, yn))],
                send_sem=side_s.at[which, i], recv_sem=side_r.at[which, i],
                device_id=peer(dx, dy), device_id_type=MESH,
            )
            c.start()
            copies.append(c)
        waits.extend(copies)
        return copies

    def gather_y(which, buf):
        copies = []
        for o in (1, 2, 3):
            c = pltpu.make_async_remote_copy(
                src_ref=buf.at[gy], dst_ref=buf.at[gy],
                send_sem=y_s.at[which, o - 1], recv_sem=y_r.at[which, o - 1],
                device_id=peer(0, o), device_id_type=MESH,
            )
            c.start()
            copies.append(c)
        waits.extend(copies)
        return copies

    def gather_x(buf, peers, send, recv):
        copies = []
        for i, o in enumerate(peers):
            c = pltpu.make_async_remote_copy(
                src_ref=buf.at[pl.ds(8 * REACH_K, 8), :], dst_ref=buf.at[pl.ds(8 * (REACH_K - o), 8), :],
                send_sem=send.at[i], recv_sem=recv.at[i],
                device_id=peer(o, 0), device_id_type=MESH,
            )
            c.start()
            copies.append(c)
        waits.extend(copies)
        return copies

    def arrive(copies):
        for c in copies:
            c.wait_recv()

    press, coef, source = w0.at[0], w0.at[1], w0.at[2]
    l0 = Level(1, 1.0, coef, r0, fx0, fy0, fz0, wt0, d0)
    l1 = Level(2, 0.25, k1, r1, fx1, fy1, fz1, wt1, d1)
    l2 = Level(4, 0.0625, k2, r2, fx2, fy2, fz2, wt2, d2)
    all0, own0 = strips(8, 88), strips(16, 80)
    all1, own1 = strips(8, 56), strips(16, 48)
    all2 = strips(8, 40)

    loads[0].wait()
    coarsen(lambda x, r, n: coef[x, pl.ds(r, n), :], 1, tmp1, k1, (8, 16, lambda j: 2 * j - 13), own0, 16)
    coarsen(lambda x, r, n: k1[x, pl.ds(r, n), :], 2, tmp2, k2, (4, 8, lambda j: 2 * j), own1, 16)
    for p, row in enumerate(pack_rows([k2[4 + i, pl.ds(16, 16), :] for i in range(4)])):
        yk[gy, pl.ds(p, 1), :] = row
    loads[1].wait()
    loads[2].wait()

    pl.semaphore_wait(barrier, len(greet))
    a_in = exchange(0, w0, w0, 3, 16, 3, 64)
    k1_in = exchange(1, k1, k1, 8, 8, 8, 32)
    yk_in = gather_y(0, yk)

    arrive(yk_in)
    for i in range(4):
        xk[pl.ds(8 * REACH_K + 2 * i, 2), :] = yk[i, pl.ds(0, 2), :]
    xk_in = gather_x(xk, PEERS_K, xk_s, xk_r)

    arrive(a_in)
    l0.inverses((0, 22), all0)
    l0.faces((0, 21), all0)
    l0.diagonal((1, 21), all0)
    l0.sweep(press, source, va0, (1, 21), all0)
    l0.sweep(va0, source, vb0, (2, 20), all0)
    coarsen(
        functools.partial(l0.residual, vb0, source), 1, tmp1, g1, (8, 16, lambda j: 2 * j - 13), own0, 16
    )
    g1_in = exchange(2, g1, g1, 8, 8, 6, 32)
    v0_in = exchange(3, vb0, vs0, 3, 16, 3, 64)

    arrive(k1_in)
    l1.inverses((0, 24), all1)
    l1.faces((0, 23), all1)
    l1.diagonal((1, 23), all1)
    coarsen(lambda x, r, n: k1[x, pl.ds(r, n), :], 2, tmp2, k2, (0, 12, lambda j: 2 * j), strips(0, 64), 8)
    l2.inverses((0, 12), all2)
    l2.faces((0, 11), all2)
    l2.diagonal((1, 11), all2)

    def keep(x):
        for r, n in own0:
            vs0[x, pl.ds(r, n), :] = vb0[x, pl.ds(r, n), :]

    loop(3, 19, keep)

    arrive(xk_in)
    shape = (SLOTS, LANES)
    pack3, pack4 = Packed3(shape), Packed4(shape)
    kk = [xk[pl.ds(i, SLOTS, stride=8), :] for i in range(8)]
    f, d = packed_coefs(pack3, kk, 1.0 / 64)
    for i in range(8):
        for j, value in enumerate((f[0][i], f[1][i], f[2][i], OMEGA * recip(d[i]), d[i])):
            c3[j, i] = value
    l, t = grid2((LANES, LANES))

    def squeeze(values):
        out = None
        for i in range(4):
            y = t // 8 - 4 * i
            choose = jnp.where((l // 32 == y) & ((l % 16) // 2 == t % 8), 0.125, 0.0).astype(F32)
            part = dot(values[2 * i] + values[2 * i + 1], choose)
            out = part if out is None else out + part
        return out

    f, d = packed_coefs(pack4, [squeeze(kk)], 1.0 / 256)
    for j, value in enumerate((f[0][0], f[1][0], f[2][0], OMEGA * recip(d[0]))):
        c4[j] = value

    arrive(g1_in)
    l1.first_sweep(g1, va1, (2, 22), all1)
    l1.sweep(va1, g1, vb1, (3, 21), all1)
    coarsen(
        functools.partial(l1.residual, vb1, g1), 2, tmp2, g2, (2, 10, lambda j: 2 * j), all1, 12
    )
    l2.first_sweep(g2, va2, (2, 10), all2)
    l2.sweep(va2, g2, vb2, (3, 9), all2)
    cells = [l2.residual(vb2, g2, 4 + i, 16, 16) for i in range(4)]
    for p, row in enumerate(pack_rows(cells)):
        yg[gy, pl.ds(p, 1), :] = row
    yg_in = gather_y(1, yg)
    for x in range(4, 8):
        w2[0, x, pl.ds(16, 16), :] = vb2[x, pl.ds(16, 16), :]
        w2[1, x, pl.ds(16, 16), :] = g2[x, pl.ds(16, 16), :]
    w2_in = exchange(4, w2, w2, 4, 4, 4, 16)
    arrive(yg_in)
    for i in range(4):
        xg[pl.ds(8 * REACH_K + 2 * i, 2), :] = yg[i, pl.ds(0, 2), :]
    xg_in = gather_x(xg, PEERS_G, xg_s, xg_r)
    arrive(xg_in)

    g3 = [xg[pl.ds(i, SLOTS, stride=8), :] for i in range(8)]
    f3 = [[c3[j, i] for i in range(8)] for j in range(3)]
    wt3 = [c3[3, i] for i in range(8)]
    saved = [a * b for a, b in zip(wt3, g3)]
    saved = packed_sweep(pack3, f3, wt3, saved, g3)
    around = pack3.both(f3, saved)
    g4 = squeeze([g3[i] + around[i] - c3[4, i] * saved[i] for i in range(8)])
    f4, wt4 = [[c4[j]] for j in range(3)], [c4[3]]

    def coarsest(_, v):
        return packed_sweep(pack4, f4, wt4, [v], [g4])[0]

    v4 = lax.fori_loop(0, 7, coarsest, wt4[0] * g4)
    v = []
    for i in range(4):
        y = l // 8 - 4 * i
        spread = jnp.where((t // 32 == y) & ((t % 16) // 2 == l % 8), 1.0, 0.0).astype(F32)
        part = dot(v4, spread)
        v += [saved[2 * i] + part, saved[2 * i + 1] + part]
    for _ in range(2):
        v = packed_sweep(pack3, f3, wt3, v, g3)
    for i in range(8):
        v3[i] = v[i]

    r, t8 = grid2((8, LANES))
    low = lax.rem(gy + (ngy - 1), ngy)
    high = lax.rem(gy + 1, ngy)
    parts = []
    for j in range(6):
        slot, p = REACH_K - 1 + j // 2, j % 2
        for part, y in ((low, 4), (gy, 0), (gy, 4), (high, 0)):
            row = jnp.broadcast_to(v3[2 * part + p, pl.ds(slot, 1), :], (8, LANES))
            parts.append(jnp.where(t8 // 16 == r // 2 + y, row, 0.0))
    spread = jnp.where(l % 16 == t // 8, 1.0, 0.0).astype(F32)
    fine = dot(jnp.concatenate(parts, axis=0), spread)
    for j in range(6):
        dup2[j] = fine[32 * j : 32 * j + 32]

    arrive(w2_in)

    def correct2(x):
        va2[x, pl.ds(8, 32), :] = w2[0, x, pl.ds(8, 32), :] + dup2[x // 2]

    loop(0, 12, correct2)
    l2.sweep(va2, w2.at[1], vb2, (1, 11), all2)
    l2.sweep(vb2, w2.at[1], va2, (2, 10), all2)

    def double2(x):
        c = va2[x, pl.ds(12, 24), :]
        dup1[x, pl.ds(8, 24, stride=2), :] = c
        dup1[x, pl.ds(9, 24, stride=2), :] = c

    loop(2, 10, double2)

    def correct1(x):
        for r, n in all1:
            va1[x, pl.ds(r, n), :] = vb1[x, pl.ds(r, n), :] + dup1[x // 2, pl.ds(r, n), :]

    loop(4, 20, correct1)
    l1.sweep(va1, g1, vb1, (5, 19), all1)
    l1.sweep(vb1, g1, va1, (6, 18), all1)

    def double1(x):
        c = va1[x, pl.ds(12, 40), :]
        tmp1[x, pl.ds(8, 40, stride=2), :] = c
        tmp1[x, pl.ds(9, 40, stride=2), :] = c

    loop(6, 18, double1)
    arrive(v0_in)
    for c in v0_in:
        c.wait_send()

    def correct0(x):
        for r, n in all0:
            va0[x, pl.ds(r, n), :] = vs0[x, pl.ds(r, n), :] + tmp1[(x + 13) // 2, pl.ds(r, n), :]

    loop(0, 22, correct0)
    l0.sweep(va0, source, vb0, (1, 21), all0)
    l0.sweep(vb0, source, va0, (2, 20), all0)
    v_store = pltpu.make_async_copy(va0.at[pl.ds(3, 16), pl.ds(16, 64), :], v_out, store_sem.at[0])
    v_store.start()

    def final(x):
        for r, n in own0:
            res0[x - 3, pl.ds(r - 16, n), :] = l0.residual(va0, source, x, r, n)

    loop(3, 19, final)
    r_store = pltpu.make_async_copy(res0, r_out, store_sem.at[1])
    r_store.start()
    done = [id(c) for c in v0_in]
    for c in waits:
        if id(c) not in done:
            c.wait_send()
    v_store.wait()
    r_store.wait()


def solution(mesh):
    ngx, ngy = mesh.shape["gx"], mesh.shape["gy"]

    def vmem(*shape):
        return pltpu.VMEM(shape, F32)

    n0, n1, n2 = (22, 96, LANES), (24, 64, LANES), (12, 48, LANES)
    scratch = [vmem(3, *n0)] + [vmem(*n0)] * 9 + [vmem(16, 64, LANES)]
    scratch += [vmem(*n1)] * 10 + [vmem(12, 64, LANES)]
    scratch += [vmem(*n2)] * 10 + [vmem(2, *n2), vmem(6, 32, LANES)]
    scratch += [vmem(18, 96, LANES), vmem(12, 64, LANES)]
    scratch += [vmem(4, 8, LANES)] * 2 + [vmem(8 * SLOTS, LANES)] * 2
    scratch += [vmem(5, 8, SLOTS, LANES), vmem(4, SLOTS, LANES), vmem(8, SLOTS, LANES)]
    dma = pltpu.SemaphoreType.DMA
    scratch += [dma((3,)), dma((2,)), dma((5, 8)), dma((5, 8)), dma((2, 3)), dma((2, 3))]
    scratch += [dma((len(PEERS_K),))] * 2 + [dma((len(PEERS_G),))] * 2

    def per_device(pressure, inverse_density, source):
        block = jax.ShapeDtypeStruct(pressure.shape, F32)
        return pl.pallas_call(
            functools.partial(kernel, ngx, ngy),
            out_shape=(block, block),
            in_specs=[pl.BlockSpec(memory_space=pl.ANY)] * 3,
            out_specs=[pl.BlockSpec(memory_space=pl.ANY)] * 2,
            scratch_shapes=scratch,
            compiler_params=pltpu.CompilerParams(
                collective_id=0, has_side_effects=True, vmem_limit_bytes=48 * 2**20
            ),
        )(pressure, inverse_density, source)

    spec = P("gx", "gy", None)
    return jax.shard_map(
        per_device, mesh=mesh, in_specs=(spec,) * 3, out_specs=(spec, spec), check_vma=False
    )
```

```python
import functools

import jax
import jax.numpy as jnp
from jax import lax
from jax.experimental import pallas as pl
from jax.experimental.pallas import tpu as pltpu
from jax.sharding import PartitionSpec as P

MESH = pl.DeviceIdType.MESH
F32 = jnp.float32
OMEGA = 0.8
LANES = 128
SIDES = ((-1, 0), (1, 0), (0, -1), (0, 1), (-1, -1), (-1, 1), (1, -1), (1, 1))
REACH_G = 10
REACH_K = 11
SLOTS = 24
PEERS_K = [o for d in range(REACH_K, 0, -1) for o in (d, -d)]
PEERS_G = [o for d in range(REACH_G, 0, -1) for o in (d, -d)]


def recip(x):
    y = pl.reciprocal(x, approx=True)
    return y * (2.0 - x * y)


def roll(x, shift, axis):
    return pltpu.roll(x, shift % x.shape[axis], axis)


def loop(lo, hi, body, most=8):
    n = hi - lo
    sizes = [u for u in range(4, most + 1) if n % u == 0]
    size = max(sizes) if sizes else -(-n // -(-n // most)) - (1 if n > most else 0)
    turns = n // size

    def step(i, carry):
        for j in range(size):
            body(lo + i * size + j)
        return carry

    if turns > 1:
        lax.fori_loop(0, turns, step, 0)
    else:
        step(0, 0)
    for i in range(lo + turns * size, hi):
        body(i)


def strips(lo, hi, size=16):
    return [(r, min(size, hi - r)) for r in range(lo, hi, size)]


def lane_index(shape):
    return lax.broadcasted_iota(jnp.int32, shape, 1)


def pair_sum_z(x, s):
    first = (lane_index(x.shape) // s) % 2 == 0
    return x + jnp.where(first, roll(x, -s, 1), roll(x, s, 1))


class Level:
    def __init__(self, s, scale, k, r, fx, fy, fz, w, d):
        self.s, self.scale, self.k = s, scale, k
        self.r, self.fx, self.fy, self.fz, self.w, self.d = r, fx, fy, fz, w, d

    def inverses(self, planes, rows):
        def body(x):
            for r, n in rows:
                self.r[x, pl.ds(r, n), :] = (0.5 / self.scale) * recip(self.k[x, pl.ds(r, n), :])

        loop(*planes, body)

    def faces(self, planes, rows):
        def body(x):
            for r, n in rows:
                here = self.r[x, pl.ds(r, n), :]
                self.fx[x, pl.ds(r, n), :] = recip(here + self.r[x + 1, pl.ds(r, n), :])
                self.fy[x, pl.ds(r, n), :] = recip(here + self.r[x, pl.ds(r + 1, n), :])
                self.fz[x, pl.ds(r, n), :] = recip(here + roll(here, -self.s, 1))

        loop(*planes, body)

    def diagonal(self, planes, rows):
        def body(x):
            for r, n in rows:
                fz = self.fz[x, pl.ds(r, n), :]
                d = self.fx[x, pl.ds(r, n), :] + self.fx[x - 1, pl.ds(r, n), :]
                d += self.fy[x, pl.ds(r, n), :] + self.fy[x, pl.ds(r - 1, n), :]
                d += fz + roll(fz, self.s, 1)
                self.d[x, pl.ds(r, n), :] = d
                self.w[x, pl.ds(r, n), :] = OMEGA * recip(d)

        loop(*planes, body)

    def around(self, v, x, r, n):
        here = v[x, pl.ds(r, n), :]
        fz = self.fz[x, pl.ds(r, n), :]
        a = self.fx[x, pl.ds(r, n), :] * v[x + 1, pl.ds(r, n), :]
        a += self.fx[x - 1, pl.ds(r, n), :] * v[x - 1, pl.ds(r, n), :]
        a += self.fy[x, pl.ds(r, n), :] * v[x, pl.ds(r + 1, n), :]
        a += self.fy[x, pl.ds(r - 1, n), :] * v[x, pl.ds(r - 1, n), :]
        a += fz * roll(here, -self.s, 1) + roll(fz * here, self.s, 1)
        return here, a

    def first_sweep(self, g, dst, planes, rows):
        def body(x):
            for r, n in rows:
                dst[x, pl.ds(r, n), :] = self.w[x, pl.ds(r, n), :] * g[x, pl.ds(r, n), :]

        loop(*planes, body)

    def sweep(self, src, g, dst, planes, rows):
        def body(x):
            for r, n in rows:
                here, a = self.around(src, x, r, n)
                w = self.w[x, pl.ds(r, n), :]
                dst[x, pl.ds(r, n), :] = (1.0 - OMEGA) * here + w * (g[x, pl.ds(r, n), :] + a)

        loop(*planes, body)

    def residual(self, v, g, x, r, n):
        here, a = self.around(v, x, r, n)
        return g[x, pl.ds(r, n), :] + a - self.d[x, pl.ds(r, n), :] * here


def coarsen(value, s, tmp, dst, pairs, rows, dst_rows):
    lo, hi, plane = pairs

    def gather(j):
        x = plane(j)
        for r, n in rows:
            tmp[j, pl.ds(r, n), :] = value(x, r, n) + value(x + 1, r, n)

    loop(lo, hi, gather)
    first, count = rows[0][0], sum(n for _, n in rows) // 2

    def squeeze(j):
        even = tmp[j, pl.ds(first, count, stride=2), :]
        odd = tmp[j, pl.ds(first + 1, count, stride=2), :]
        dst[j, pl.ds(dst_rows, count), :] = 0.125 * pair_sum_z(even + odd, s)

    loop(lo, hi, squeeze)


class Packed3:
    def __init__(self, shape):
        lane = lane_index(shape)
        self.y_last, self.y_first = lane >= 112, lane < 16
        self.z_last, self.z_first = lane % 16 == 15, lane % 16 == 0

    def y_next(self, v):
        t = [roll(a, -16, 1) for a in v]
        return [jnp.where(self.y_last, t[(i + 2) % 8], t[i]) for i in range(8)]

    def y_prev(self, v):
        t = [roll(a, 16, 1) for a in v]
        return [jnp.where(self.y_first, t[(i - 2) % 8], t[i]) for i in range(8)]

    def z_next(self, v):
        return [jnp.where(self.z_last, roll(a, 15, 1), roll(a, -1, 1)) for a in v]

    def z_prev(self, v):
        return [jnp.where(self.z_first, roll(a, -15, 1), roll(a, 1, 1)) for a in v]

    def x_next(self, v):
        return [v[i + 1] if i % 2 == 0 else roll(v[i - 1], -1, 0) for i in range(8)]

    def x_prev(self, v):
        return [roll(v[i + 1], 1, 0) if i % 2 == 0 else v[i - 1] for i in range(8)]

    def both(self, f, v):
        out = None
        for axis in range(3):
            nxt = (self.x_next, self.y_next, self.z_next)[axis](v)
            prv = (self.x_prev, self.y_prev, self.z_prev)[axis]([a * b for a, b in zip(f[axis], v)])
            term = [a * b + c for a, b, c in zip(f[axis], nxt, prv)]
            out = term if out is None else [a + b for a, b in zip(out, term)]
        return out


class Packed4(Packed3):
    def __init__(self, shape):
        lane = lane_index(shape)
        self.z_last, self.z_first = lane % 8 == 7, lane % 8 == 0

    def y_next(self, v):
        return [roll(v[0], -8, 1)]

    def y_prev(self, v):
        return [roll(v[0], 8, 1)]

    def z_next(self, v):
        return [jnp.where(self.z_last, roll(v[0], 7, 1), roll(v[0], -1, 1))]

    def z_prev(self, v):
        return [jnp.where(self.z_first, roll(v[0], -7, 1), roll(v[0], 1, 1))]

    def x_next(self, v):
        return [roll(v[0], -1, 0)]

    def x_prev(self, v):
        return [roll(v[0], 1, 0)]


def packed_coefs(pack, k, scale):
    r = [(0.5 / scale) * recip(a) for a in k]
    f = []
    d = None
    for nxt, prv in ((pack.x_next, pack.x_prev), (pack.y_next, pack.y_prev), (pack.z_next, pack.z_prev)):
        face = [recip(a + b) for a, b in zip(r, nxt(r))]
        f.append(face)
        both = [a + b for a, b in zip(face, prv(face))]
        d = both if d is None else [a + b for a, b in zip(d, both)]
    return f, d


def packed_sweep(pack, f, w, v, g):
    return [
        (1.0 - OMEGA) * a + b * (c + e) for a, b, c, e in zip(v, w, g, pack.both(f, v))
    ]


def dot(a, b):
    return jnp.dot(a, b, precision=lax.Precision.HIGHEST, preferred_element_type=F32)


def grid2(shape):
    return lax.broadcasted_iota(jnp.int32, shape, 0), lax.broadcasted_iota(jnp.int32, shape, 1)


def pack_rows(cells):
    l, t = grid2((LANES, LANES))
    choose = jnp.where((l // 8 == t % 16) & (l % 4 == 0), 0.125, 0.0).astype(F32)
    r, t = grid2((16, LANES))
    keep = r // 2 == t // 16
    rows = []
    for p in range(2):
        u = dot(cells[2 * p] + cells[2 * p + 1], choose)
        rows.append(jnp.sum(jnp.where(keep, u, 0.0), axis=0, keepdims=True))
    return rows


def kernel(
    ngx, ngy, p_hbm, k_hbm, s_hbm, v_out, r_out,
    w0, r0, fx0, fy0, fz0, wt0, d0, va0, vb0, vs0, res0,
    k1, r1, fx1, fy1, fz1, wt1, d1, g1, va1, vb1, dup1,
    k2, r2, fx2, fy2, fz2, wt2, d2, g2, va2, vb2, w2, dup2,
    tmp1, tmp2, yk, yg, xk, xg, c3, c4, v3,
    load_sem, store_sem, side_s, side_r, y_s, y_r, xk_s, xk_r, xg_s, xg_r,
):
    gx, gy = lax.axis_index("gx"), lax.axis_index("gy")

    def peer(dx, dy):
        return (lax.rem(gx + (dx + ngx), ngx), lax.rem(gy + (dy + ngy), ngy))

    loads = [
        pltpu.make_async_copy(hbm, w0.at[i, pl.ds(3, 16), pl.ds(16, 64), :], load_sem.at[i])
        for i, hbm in ((1, k_hbm), (0, p_hbm), (2, s_hbm))
    ]
    for c in loads:
        c.start()

    greet = [(o, 0) for o in PEERS_K if abs(o) > 1] + [(0, 2)] + list(SIDES)[::-1]
    barrier = pltpu.get_barrier_semaphore()
    for o in greet:
        pl.semaphore_signal(barrier, inc=1, device_id=peer(*o), device_id_type=MESH)

    waits = []

    def exchange(which, src, dst, x0, nx, hx, ny, hy):
        y0 = 16
        lead = (slice(None),) * (len(src.shape) - 3)
        copies = []
        for i, (dx, dy) in enumerate(SIDES):
            xs, xd, xn = ((x0, x0 + nx, hx), (x0, x0, nx), (x0 + nx - hx, x0 - hx, hx))[dx + 1]
            ys, yd, yn = ((y0, y0 + ny, hy), (y0, y0, ny), (y0 + ny - hy, y0 - hy, hy))[dy + 1]
            c = pltpu.make_async_remote_copy(
                src_ref=src.at[lead + (pl.ds(xs, xn), pl.ds(ys, yn))],
                dst_ref=dst.at[lead + (pl.ds(xd, xn), pl.ds(yd, yn))],
                send_sem=side_s.at[which, i], recv_sem=side_r.at[which, i],
                device_id=peer(dx, dy), device_id_type=MESH,
            )
            c.start()
            copies.append(c)
        waits.extend(copies)
        return copies

    def gather_y(which, buf):
        copies = []
        for o in (1, 2, 3):
            c = pltpu.make_async_remote_copy(
                src_ref=buf.at[gy], dst_ref=buf.at[gy],
                send_sem=y_s.at[which, o - 1], recv_sem=y_r.at[which, o - 1],
                device_id=peer(0, o), device_id_type=MESH,
            )
            c.start()
            copies.append(c)
        waits.extend(copies)
        return copies

    def gather_x(buf, peers, send, recv):
        copies = []
        for i, o in enumerate(peers):
            c = pltpu.make_async_remote_copy(
                src_ref=buf.at[pl.ds(8 * REACH_K, 8), :], dst_ref=buf.at[pl.ds(8 * (REACH_K - o), 8), :],
                send_sem=send.at[i], recv_sem=recv.at[i],
                device_id=peer(o, 0), device_id_type=MESH,
            )
            c.start()
            copies.append(c)
        waits.extend(copies)
        return copies

    def arrive(copies):
        for c in copies:
            c.wait_recv()

    press, coef, source = w0.at[0], w0.at[1], w0.at[2]
    l0 = Level(1, 1.0, coef, r0, fx0, fy0, fz0, wt0, d0)
    l1 = Level(2, 0.25, k1, r1, fx1, fy1, fz1, wt1, d1)
    l2 = Level(4, 0.0625, k2, r2, fx2, fy2, fz2, wt2, d2)
    all0, own0, mid0, rim0 = strips(8, 88), strips(16, 80), strips(24, 72), [(8, 16), (72, 16)]
    all1, own1 = strips(8, 56), strips(16, 48)
    all2 = strips(8, 40)

    for c in loads:
        c.wait()
    pl.semaphore_wait(barrier, len(greet))
    a_in = exchange(0, w0, w0, 3, 16, 3, 64, 3)
    coarsen(lambda x, r, n: coef[x, pl.ds(r, n), :], 1, tmp1, k1, (8, 16, lambda j: 2 * j - 13), own0, 16)
    coarsen(lambda x, r, n: k1[x, pl.ds(r, n), :], 2, tmp2, k2, (4, 8, lambda j: 2 * j), own1, 16)
    for p, row in enumerate(pack_rows([k2[4 + i, pl.ds(16, 16), :] for i in range(4)])):
        yk[gy, pl.ds(p, 1), :] = row
    k1_in = exchange(1, k1, k1, 8, 8, 8, 32, 8)
    yk_in = gather_y(0, yk)

    l0.inverses((3, 19), own0)
    l0.faces((3, 18), own0)
    l0.diagonal((4, 18), mid0)
    l0.sweep(press, source, va0, (4, 18), mid0)

    arrive(a_in)
    for planes in ((0, 3), (19, 22)):
        l0.inverses(planes, all0)
    l0.inverses((3, 19), [(8, 8), (80, 8)])
    for planes in ((0, 3), (18, 21)):
        l0.faces(planes, all0)
    l0.faces((3, 18), [(8, 8), (72, 16)])
    for planes in ((1, 4), (18, 21)):
        l0.diagonal(planes, all0)
    l0.diagonal((4, 18), rim0)
    for planes in ((1, 4), (18, 21)):
        l0.sweep(press, source, va0, planes, all0)
    l0.sweep(press, source, va0, (4, 18), rim0)
    l0.sweep(va0, source, vb0, (2, 20), all0)
    coarsen(
        functools.partial(l0.residual, vb0, source), 1, tmp1, g1, (8, 16, lambda j: 2 * j - 13), own0, 16
    )
    g1_in = exchange(2, g1, g1, 8, 8, 6, 32, 8)
    arrive(yk_in)
    for i in range(4):
        xk[pl.ds(8 * REACH_K + 2 * i, 2), :] = yk[i, pl.ds(0, 2), :]
    xk_in = gather_x(xk, PEERS_K, xk_s, xk_r)

    arrive(k1_in)
    l1.inverses((0, 24), all1)
    l1.faces((0, 23), all1)
    l1.diagonal((1, 23), all1)
    coarsen(lambda x, r, n: k1[x, pl.ds(r, n), :], 2, tmp2, k2, (0, 12, lambda j: 2 * j), strips(0, 64), 8)
    l2.inverses((0, 12), all2)
    l2.faces((0, 11), all2)
    l2.diagonal((1, 11), all2)

    def keep(x):
        for r, n in own0:
            vs0[x, pl.ds(r, n), :] = vb0[x, pl.ds(r, n), :]

    loop(3, 19, keep)

    arrive(g1_in)
    v0_in = exchange(3, vb0, vs0, 3, 16, 3, 64, 3)
    l1.first_sweep(g1, va1, (2, 22), all1)
    l1.sweep(va1, g1, vb1, (3, 21), all1)
    coarsen(
        functools.partial(l1.residual, vb1, g1), 2, tmp2, g2, (2, 10, lambda j: 2 * j), all1, 12
    )
    l2.first_sweep(g2, va2, (2, 10), all2)
    l2.sweep(va2, g2, vb2, (3, 9), all2)
    cells = [l2.residual(vb2, g2, 4 + i, 16, 16) for i in range(4)]
    for p, row in enumerate(pack_rows(cells)):
        yg[gy, pl.ds(p, 1), :] = row
    yg_in = gather_y(1, yg)
    for x in range(4, 8):
        w2[0, x, pl.ds(16, 16), :] = vb2[x, pl.ds(16, 16), :]
        w2[1, x, pl.ds(16, 16), :] = g2[x, pl.ds(16, 16), :]
    w2_in = exchange(4, w2, w2, 4, 4, 4, 16, 8)
    arrive(xk_in)
    shape = (SLOTS, LANES)
    pack3, pack4 = Packed3(shape), Packed4(shape)
    kk = [xk[pl.ds(i, SLOTS, stride=8), :] for i in range(8)]
    f, d = packed_coefs(pack3, kk, 1.0 / 64)
    for i in range(8):
        for j, value in enumerate((f[0][i], f[1][i], f[2][i], OMEGA * recip(d[i]), d[i])):
            c3[j, i] = value
    l, t = grid2((LANES, LANES))

    def squeeze(values):
        out = None
        for i in range(4):
            y = t // 8 - 4 * i
            choose = jnp.where((l // 32 == y) & ((l % 16) // 2 == t % 8), 0.125, 0.0).astype(F32)
            part = dot(values[2 * i] + values[2 * i + 1], choose)
            out = part if out is None else out + part
        return out

    f, d = packed_coefs(pack4, [squeeze(kk)], 1.0 / 256)
    for j, value in enumerate((f[0][0], f[1][0], f[2][0], OMEGA * recip(d[0]))):
        c4[j] = value

    arrive(yg_in)
    for i in range(4):
        xg[pl.ds(8 * REACH_K + 2 * i, 2), :] = yg[i, pl.ds(0, 2), :]
    xg_in = gather_x(xg, PEERS_G, xg_s, xg_r)
    arrive(xg_in)

    g3 = [xg[pl.ds(i, SLOTS, stride=8), :] for i in range(8)]
    f3 = [[c3[j, i] for i in range(8)] for j in range(3)]
    wt3 = [c3[3, i] for i in range(8)]
    saved = [a * b for a, b in zip(wt3, g3)]
    saved = packed_sweep(pack3, f3, wt3, saved, g3)
    around = pack3.both(f3, saved)
    g4 = squeeze([g3[i] + around[i] - c3[4, i] * saved[i] for i in range(8)])
    f4, wt4 = [[c4[j]] for j in range(3)], [c4[3]]

    def coarsest(_, v):
        return packed_sweep(pack4, f4, wt4, [v], [g4])[0]

    v4 = lax.fori_loop(0, 7, coarsest, wt4[0] * g4)
    v = []
    for i in range(4):
        y = l // 8 - 4 * i
        spread = jnp.where((t // 32 == y) & ((t % 16) // 2 == l % 8), 1.0, 0.0).astype(F32)
        part = dot(v4, spread)
        v += [saved[2 * i] + part, saved[2 * i + 1] + part]
    for _ in range(2):
        v = packed_sweep(pack3, f3, wt3, v, g3)
    for i in range(8):
        v3[i] = v[i]

    r, t8 = grid2((8, LANES))
    low = lax.rem(gy + (ngy - 1), ngy)
    high = lax.rem(gy + 1, ngy)
    parts = []
    for j in range(6):
        slot, p = REACH_K - 1 + j // 2, j % 2
        for part, y in ((low, 4), (gy, 0), (gy, 4), (high, 0)):
            row = jnp.broadcast_to(v3[2 * part + p, pl.ds(slot, 1), :], (8, LANES))
            parts.append(jnp.where(t8 // 16 == r // 2 + y, row, 0.0))
    spread = jnp.where(l % 16 == t // 8, 1.0, 0.0).astype(F32)
    fine = dot(jnp.concatenate(parts, axis=0), spread)
    for j in range(6):
        dup2[j] = fine[32 * j : 32 * j + 32]

    arrive(w2_in)

    def correct2(x):
        va2[x, pl.ds(8, 32), :] = w2[0, x, pl.ds(8, 32), :] + dup2[x // 2]

    loop(0, 12, correct2)
    l2.sweep(va2, w2.at[1], vb2, (1, 11), all2)
    l2.sweep(vb2, w2.at[1], va2, (2, 10), all2)

    def double2(x):
        c = va2[x, pl.ds(12, 24), :]
        dup1[x, pl.ds(8, 24, stride=2), :] = c
        dup1[x, pl.ds(9, 24, stride=2), :] = c

    loop(2, 10, double2)

    def correct1(x):
        for r, n in all1:
            va1[x, pl.ds(r, n), :] = vb1[x, pl.ds(r, n), :] + dup1[x // 2, pl.ds(r, n), :]

    loop(4, 20, correct1)
    l1.sweep(va1, g1, vb1, (5, 19), all1)
    l1.sweep(vb1, g1, va1, (6, 18), all1)

    def double1(x):
        c = va1[x, pl.ds(12, 40), :]
        tmp1[x, pl.ds(8, 40, stride=2), :] = c
        tmp1[x, pl.ds(9, 40, stride=2), :] = c

    loop(6, 18, double1)
    arrive(v0_in)
    for c in v0_in:
        c.wait_send()

    def correct0(x):
        for r, n in all0:
            va0[x, pl.ds(r, n), :] = vs0[x, pl.ds(r, n), :] + tmp1[(x + 13) // 2, pl.ds(r, n), :]

    loop(0, 22, correct0)
    l0.sweep(va0, source, vb0, (1, 21), all0)
    l0.sweep(vb0, source, va0, (2, 20), all0)
    v_store = pltpu.make_async_copy(va0.at[pl.ds(3, 16), pl.ds(16, 64), :], v_out, store_sem.at[0])
    v_store.start()

    def final(x):
        for r, n in own0:
            res0[x - 3, pl.ds(r - 16, n), :] = l0.residual(va0, source, x, r, n)

    loop(3, 19, final)
    r_store = pltpu.make_async_copy(res0, r_out, store_sem.at[1])
    r_store.start()
    done = [id(c) for c in v0_in]
    for c in waits:
        if id(c) not in done:
            c.wait_send()
    v_store.wait()
    r_store.wait()


def solution(mesh):
    ngx, ngy = mesh.shape["gx"], mesh.shape["gy"]

    def vmem(*shape):
        return pltpu.VMEM(shape, F32)

    n0, n1, n2 = (22, 96, LANES), (24, 64, LANES), (12, 48, LANES)
    scratch = [vmem(3, *n0)] + [vmem(*n0)] * 9 + [vmem(16, 64, LANES)]
    scratch += [vmem(*n1)] * 10 + [vmem(12, 64, LANES)]
    scratch += [vmem(*n2)] * 10 + [vmem(2, *n2), vmem(6, 32, LANES)]
    scratch += [vmem(18, 96, LANES), vmem(12, 64, LANES)]
    scratch += [vmem(4, 8, LANES)] * 2 + [vmem(8 * SLOTS, LANES)] * 2
    scratch += [vmem(5, 8, SLOTS, LANES), vmem(4, SLOTS, LANES), vmem(8, SLOTS, LANES)]
    dma = pltpu.SemaphoreType.DMA
    scratch += [dma((3,)), dma((2,)), dma((5, 8)), dma((5, 8)), dma((2, 3)), dma((2, 3))]
    scratch += [dma((len(PEERS_K),))] * 2 + [dma((len(PEERS_G),))] * 2

    def per_device(pressure, inverse_density, source):
        block = jax.ShapeDtypeStruct(pressure.shape, F32)
        return pl.pallas_call(
            functools.partial(kernel, ngx, ngy),
            out_shape=(block, block),
            in_specs=[pl.BlockSpec(memory_space=pltpu.HBM)] * 3,
            out_specs=[pl.BlockSpec(memory_space=pl.ANY)] * 2,
            scratch_shapes=scratch,
            compiler_params=pltpu.CompilerParams(
                collective_id=0, has_side_effects=True, vmem_limit_bytes=105 * 2**19
            ),
        )(pressure, inverse_density, source)

    spec = P("gx", "gy", None)
    return jax.shard_map(
        per_device, mesh=mesh, in_specs=(spec,) * 3, out_specs=(spec, spec), check_vma=False
    )
```

```python
import functools

import jax
import jax.numpy as jnp
from jax import lax
from jax.experimental import pallas as pl
from jax.experimental.pallas import tpu as pltpu
from jax.sharding import PartitionSpec as P

MESH = pl.DeviceIdType.MESH
F32 = jnp.float32
BF16 = jnp.bfloat16
OMEGA = 0.8
LANES = 128
SIDES = ((-1, 0), (1, 0), (0, -1), (0, 1), (-1, -1), (-1, 1), (1, -1), (1, 1))
SLOTS = 24
CHIPS = [c for d in range(5, 0, -1) for c in (d, -d)]


def recip(x):
    y = pl.reciprocal(x, approx=True)
    return y * (2.0 - x * y)


def roll(x, shift, axis):
    return pltpu.roll(x, shift % x.shape[axis], axis)


def loop(lo, hi, body, most=8):
    n = hi - lo
    sizes = [u for u in range(4, most + 1) if n % u == 0]
    size = max(sizes) if sizes else -(-n // -(-n // most)) - (1 if n > most else 0)
    turns = n // size

    def step(i, carry):
        for j in range(size):
            body(lo + i * size + j)
        return carry

    if turns > 1:
        lax.fori_loop(0, turns, step, 0)
    else:
        step(0, 0)
    for i in range(lo + turns * size, hi):
        body(i)


def strips(lo, hi, size=16):
    return [(r, min(size, hi - r)) for r in range(lo, hi, size)]


def lane_index(shape):
    return lax.broadcasted_iota(jnp.int32, shape, 1)


def pair_sum_z(x, s):
    first = (lane_index(x.shape) // s) % 2 == 0
    return x + jnp.where(first, roll(x, -s, 1), roll(x, s, 1))


class Level:
    def __init__(self, s, scale, k, r, fx, fy, fz, w, d):
        self.s, self.scale, self.k = s, scale, k
        self.r, self.fx, self.fy, self.fz, self.w, self.d = r, fx, fy, fz, w, d

    def inverses(self, planes, rows):
        def body(x):
            for r, n in rows:
                self.r[x, pl.ds(r, n), :] = (0.5 / self.scale) * recip(self.k[x, pl.ds(r, n), :])

        loop(*planes, body)

    def faces(self, planes, rows):
        def body(x):
            for r, n in rows:
                here = self.r[x, pl.ds(r, n), :]
                self.fx[x, pl.ds(r, n), :] = recip(here + self.r[x + 1, pl.ds(r, n), :])
                self.fy[x, pl.ds(r, n), :] = recip(here + self.r[x, pl.ds(r + 1, n), :])
                self.fz[x, pl.ds(r, n), :] = recip(here + roll(here, -self.s, 1))

        loop(*planes, body)

    def diagonal(self, planes, rows):
        def body(x):
            for r, n in rows:
                fz = self.fz[x, pl.ds(r, n), :]
                d = self.fx[x, pl.ds(r, n), :] + self.fx[x - 1, pl.ds(r, n), :]
                d += self.fy[x, pl.ds(r, n), :] + self.fy[x, pl.ds(r - 1, n), :]
                d += fz + roll(fz, self.s, 1)
                self.d[x, pl.ds(r, n), :] = d
                self.w[x, pl.ds(r, n), :] = OMEGA * recip(d)

        loop(*planes, body)

    def around(self, v, x, r, n):
        here = v[x, pl.ds(r, n), :]
        fz = self.fz[x, pl.ds(r, n), :]
        a = self.fx[x, pl.ds(r, n), :] * v[x + 1, pl.ds(r, n), :]
        a += self.fx[x - 1, pl.ds(r, n), :] * v[x - 1, pl.ds(r, n), :]
        a += self.fy[x, pl.ds(r, n), :] * v[x, pl.ds(r + 1, n), :]
        a += self.fy[x, pl.ds(r - 1, n), :] * v[x, pl.ds(r - 1, n), :]
        a += fz * roll(here, -self.s, 1) + roll(fz * here, self.s, 1)
        return here, a

    def first_sweep(self, g, dst, planes, rows):
        def body(x):
            for r, n in rows:
                dst[x, pl.ds(r, n), :] = self.w[x, pl.ds(r, n), :] * g[x, pl.ds(r, n), :]

        loop(*planes, body)

    def sweep(self, src, g, dst, planes, rows):
        def body(x):
            for r, n in rows:
                here, a = self.around(src, x, r, n)
                w = self.w[x, pl.ds(r, n), :]
                dst[x, pl.ds(r, n), :] = (1.0 - OMEGA) * here + w * (g[x, pl.ds(r, n), :] + a)

        loop(*planes, body)

    def residual(self, v, g, x, r, n):
        here, a = self.around(v, x, r, n)
        return g[x, pl.ds(r, n), :] + a - self.d[x, pl.ds(r, n), :] * here


def add_planes(value, tmp, pairs, rows):
    lo, hi, plane = pairs

    def gather(j):
        x = plane(j)
        for r, n in rows:
            tmp[j, pl.ds(r, n), :] = value(x, r, n) + value(x + 1, r, n)

    loop(lo, hi, gather)


def coarsen(value, s, tmp, dst, pairs, rows, dst_rows, parts=None):
    lo, hi, plane = pairs
    for part_lo, part_hi, part_rows in parts or [(lo, hi, rows)]:
        add_planes(value, tmp, (part_lo, part_hi, plane), part_rows)
    first, count = rows[0][0], sum(n for _, n in rows) // 2

    def squeeze(j):
        even = tmp[j, pl.ds(first, count, stride=2), :]
        odd = tmp[j, pl.ds(first + 1, count, stride=2), :]
        dst[j, pl.ds(dst_rows, count), :] = 0.125 * pair_sum_z(even + odd, s)

    loop(lo, hi, squeeze)


class Packed3:
    def __init__(self, shape):
        lane = lane_index(shape)
        self.y_last, self.y_first = lane >= 112, lane < 16
        self.z_last, self.z_first = lane % 16 == 15, lane % 16 == 0

    def y_next(self, v):
        t = [roll(a, -16, 1) for a in v]
        return [jnp.where(self.y_last, t[(i + 2) % 8], t[i]) for i in range(8)]

    def y_prev(self, v):
        t = [roll(a, 16, 1) for a in v]
        return [jnp.where(self.y_first, t[(i - 2) % 8], t[i]) for i in range(8)]

    def z_next(self, v):
        return [jnp.where(self.z_last, roll(a, 15, 1), roll(a, -1, 1)) for a in v]

    def z_prev(self, v):
        return [jnp.where(self.z_first, roll(a, -15, 1), roll(a, 1, 1)) for a in v]

    def x_next(self, v):
        return [v[i + 1] if i % 2 == 0 else roll(v[i - 1], -1, 0) for i in range(8)]

    def x_prev(self, v):
        return [roll(v[i + 1], 1, 0) if i % 2 == 0 else v[i - 1] for i in range(8)]

    def both(self, f, v):
        out = None
        for axis in range(3):
            nxt = (self.x_next, self.y_next, self.z_next)[axis](v)
            prv = (self.x_prev, self.y_prev, self.z_prev)[axis]([a * b for a, b in zip(f[axis], v)])
            term = [a * b + c for a, b, c in zip(f[axis], nxt, prv)]
            out = term if out is None else [a + b for a, b in zip(out, term)]
        return out


class Packed4(Packed3):
    def __init__(self, shape):
        lane = lane_index(shape)
        self.z_last, self.z_first = lane % 8 == 7, lane % 8 == 0

    def y_next(self, v):
        return [roll(v[0], -8, 1)]

    def y_prev(self, v):
        return [roll(v[0], 8, 1)]

    def z_next(self, v):
        return [jnp.where(self.z_last, roll(v[0], 7, 1), roll(v[0], -1, 1))]

    def z_prev(self, v):
        return [jnp.where(self.z_first, roll(v[0], -7, 1), roll(v[0], 1, 1))]

    def x_next(self, v):
        return [roll(v[0], -1, 0)]

    def x_prev(self, v):
        return [roll(v[0], 1, 0)]


def packed_coefs(pack, k, scale):
    r = [(0.5 / scale) * recip(a) for a in k]
    f = []
    d = None
    for nxt, prv in ((pack.x_next, pack.x_prev), (pack.y_next, pack.y_prev), (pack.z_next, pack.z_prev)):
        face = [recip(a + b) for a, b in zip(r, nxt(r))]
        f.append(face)
        both = [a + b for a, b in zip(face, prv(face))]
        d = both if d is None else [a + b for a, b in zip(d, both)]
    return f, d


def packed_sweep(pack, f, w, v, g):
    return [
        (1.0 - OMEGA) * a + b * (c + e) for a, b, c, e in zip(v, w, g, pack.both(f, v))
    ]


def dot(a, choose):
    out = None
    for _ in range(3):
        part = a.astype(BF16)
        a = a - part.astype(F32)
        term = jnp.dot(part, choose, preferred_element_type=F32)
        out = term if out is None else out + term
    return out


def grid2(shape):
    return lax.broadcasted_iota(jnp.int32, shape, 0), lax.broadcasted_iota(jnp.int32, shape, 1)


def pack_rows(cells):
    l, t = grid2((LANES, LANES))
    choose = jnp.where((l // 8 == t % 16) & (l % 4 == 0), 0.125, 0.0).astype(BF16)
    r, t = grid2((16, LANES))
    keep = r // 2 == t // 16
    rows = []
    for p in range(2):
        u = dot(cells[2 * p] + cells[2 * p + 1], choose)
        rows.append(jnp.sum(jnp.where(keep, u, 0.0), axis=0, keepdims=True))
    return rows


def kernel(
    ngx, ngy, p_hbm, k_hbm, s_hbm, v_out, r_out,
    w0, r0, fx0, fy0, fz0, wt0, d0, va0, vb0, vs0, res0,
    k1, r1, fx1, fy1, fz1, wt1, d1, g1, va1, vb1, dup1,
    k2, r2, fx2, fy2, fz2, wt2, d2, g2, va2, vb2, w2, dup2,
    tmp1, tmp2, tmp0, yk, yg, xk, xg, c3, c4, v3,
    load_sem, store_sem, side_s, side_r, gather_sem,
):
    gx, gy = lax.axis_index("gx"), lax.axis_index("gy")
    parity = lax.rem(gx, 2)

    def peer(dx, dy):
        return (lax.rem(gx + (dx + ngx), ngx), lax.rem(gy + (dy + ngy), ngy))

    loads = [
        pltpu.make_async_copy(hbm, w0.at[i, pl.ds(3, 16), pl.ds(16, 64), :], load_sem.at[i])
        for i, hbm in ((1, k_hbm), (0, p_hbm), (2, s_hbm))
    ]
    for c in loads:
        c.start()

    greet = [(2 * c, 0) for c in (6, -6, *CHIPS)] + [(0, 2), (1 - 2 * parity, 2)] + list(SIDES)[::-1]
    barrier = pltpu.get_barrier_semaphore()
    for o in greet:
        pl.semaphore_signal(barrier, inc=1, device_id=peer(*o), device_id_type=MESH)

    waits = []

    def exchange(which, src, dst, x0, nx, hx, ny, hy):
        y0 = 16
        lead = (slice(None),) * (len(src.shape) - 3)
        copies = []
        for i, (dx, dy) in enumerate(SIDES):
            xs, xd, xn = ((x0, x0 + nx, hx), (x0, x0, nx), (x0 + nx - hx, x0 - hx, hx))[dx + 1]
            ys, yd, yn = ((y0, y0 + ny, hy), (y0, y0, ny), (y0 + ny - hy, y0 - hy, hy))[dy + 1]
            c = pltpu.make_async_remote_copy(
                src_ref=src.at[lead + (pl.ds(xs, xn), pl.ds(ys, yn))],
                dst_ref=dst.at[lead + (pl.ds(xd, xn), pl.ds(yd, yn))],
                send_sem=side_s.at[which, i], recv_sem=side_r.at[which, i],
                device_id=peer(dx, dy), device_id_type=MESH,
            )
            c.start()
            copies.append(c)
        waits.extend(copies)
        return copies

    def wait_all(buf, tiles, send, recv):
        every = buf.at[pl.ds(0, 8 * tiles), :]
        c = pltpu.make_async_remote_copy(
            src_ref=every, dst_ref=every, send_sem=send, recv_sem=recv,
            device_id=peer(1, 0), device_id_type=MESH,
        )
        waits.append(c)
        return [c]

    def gather_near(buf, send, recv):
        mine = pl.ds(pl.multiple_of(8 * (4 * parity + gy), 8), 8)
        for dx, dy in ((1, 2), (0, 2), (1, 1), (1, 3), (0, 1), (0, 3), (1, 0)):
            c = pltpu.make_async_remote_copy(
                src_ref=buf.at[mine, :], dst_ref=buf.at[mine, :], send_sem=send, recv_sem=recv,
                device_id=peer(dx * (1 - 2 * parity), dy), device_id_type=MESH,
            )
            c.start()
        return wait_all(buf, 7, send, recv)

    def chip_rows(c):
        return pl.ds(pl.multiple_of(16 * (6 + c - parity), 16), 16)

    def gather_x(buf, chips, send, recv):
        for c in chips:
            copy = pltpu.make_async_remote_copy(
                src_ref=buf.at[chip_rows(0), :], dst_ref=buf.at[chip_rows(-c), :], send_sem=send, recv_sem=recv,
                device_id=peer(2 * c, 0), device_id_type=MESH,
            )
            copy.start()
        return wait_all(buf, 2 * len(chips), send, recv)

    def assemble(near, buf):
        for device in range(2):
            for i in range(4):
                row = pl.multiple_of(8 * (2 * (6 - parity) + device), 8) + 2 * i
                buf[pl.ds(row, 2), :] = near[pl.ds(8 * (4 * device + i), 2), :]

    def arrive(copies):
        for c in copies:
            c.wait_recv()

    def sent(keep=0):
        count = len(waits) - keep
        for c in waits[:count]:
            c.wait_send()
        del waits[:count]

    press, coef, source = w0.at[0], w0.at[1], w0.at[2]
    l0 = Level(1, 1.0, coef, r0, fx0, fy0, fz0, wt0, d0)
    l1 = Level(2, 0.25, k1, r1, fx1, fy1, fz1, wt1, d1)
    l2 = Level(4, 0.0625, k2, r2, fx2, fy2, fz2, wt2, d2)
    all0, own0, mid0, rim0 = strips(8, 88), strips(16, 80), strips(24, 72), [(8, 16), (72, 16)]
    all1, own1 = strips(8, 56), strips(16, 48)
    all2 = strips(8, 40)

    for c in loads:
        c.wait()
    pl.semaphore_wait(barrier, len(greet))
    coef_in = exchange(0, coef, coef, 3, 16, 3, 64, 3)
    press_in = exchange(5, press, press, 3, 16, 3, 64, 3)
    source_in = exchange(6, source, source, 3, 16, 2, 64, 2)
    coarsen(lambda x, r, n: coef[x, pl.ds(r, n), :], 1, tmp1, k1, (8, 16, lambda j: 2 * j - 13), own0, 16)
    coarsen(lambda x, r, n: k1[x, pl.ds(r, n), :], 2, tmp2, k2, (4, 8, lambda j: 2 * j), own1, 16)
    for p, row in enumerate(pack_rows([k2[4 + i, pl.ds(16, 16), :] for i in range(4)])):
        yk[pl.ds(8 * (4 * parity + gy) + p, 1), :] = row
    k1_in = exchange(1, k1, k1, 8, 8, 8, 32, 8)
    yk_in = gather_near(yk, gather_sem.at[0], gather_sem.at[1])

    l0.inverses((3, 19), own0)
    l0.faces((3, 18), own0)
    l0.diagonal((4, 18), own0)
    l0.sweep(press, source, va0, (4, 18), [(17, 7), *mid0, (72, 7)])
    l0.sweep(va0, source, vb0, (5, 17), mid0)
    residual0 = functools.partial(l0.residual, vb0, source)
    add_planes(residual0, tmp0, (10, 14, lambda j: 2 * j - 13), strips(32, 64))

    arrive(coef_in)
    for planes in ((0, 3), (19, 22)):
        l0.inverses(planes, all0)
    l0.inverses((3, 19), [(8, 8), (80, 8)])
    for planes in ((0, 3), (18, 21)):
        l0.faces(planes, all0)
    l0.faces((3, 18), [(8, 8), (72, 16)])
    for planes in ((1, 4), (18, 21)):
        l0.diagonal(planes, all0)
    l0.diagonal((4, 18), rim0)
    arrive(press_in)
    arrive(source_in)
    for planes in ((1, 4), (18, 21)):
        l0.sweep(press, source, va0, planes, all0)
    l0.sweep(press, source, va0, (4, 18), rim0)
    for planes in ((2, 5), (17, 20)):
        l0.sweep(va0, source, vb0, planes, all0)
    l0.sweep(va0, source, vb0, (5, 17), rim0)
    edge0 = [(16, 16), (64, 16)]
    coarsen(
        residual0, 1, tmp0, g1, (8, 16, lambda j: 2 * j - 13), own0, 16,
        [(8, 10, own0), (10, 14, edge0), (14, 16, own0)],
    )
    g1_in = exchange(2, g1, g1, 8, 8, 6, 32, 8)
    arrive(yk_in)
    assemble(yk, xk)
    xk_in = gather_x(xk, [6 - 12 * parity, *CHIPS], gather_sem.at[4], gather_sem.at[5])

    arrive(k1_in)
    l1.inverses((0, 24), all1)
    l1.faces((0, 23), all1)
    l1.diagonal((1, 23), all1)
    coarsen(lambda x, r, n: k1[x, pl.ds(r, n), :], 2, tmp2, k2, (0, 12, lambda j: 2 * j), strips(0, 64), 8)
    l2.inverses((0, 12), all2)
    l2.faces((0, 11), all2)
    l2.diagonal((1, 11), all2)

    def keep(x):
        for r, n in own0:
            vs0[x, pl.ds(r, n), :] = vb0[x, pl.ds(r, n), :]

    loop(3, 19, keep)

    arrive(g1_in)
    v0_in = exchange(3, vb0, vs0, 3, 16, 3, 64, 3)
    l1.first_sweep(g1, va1, (2, 22), all1)
    l1.sweep(va1, g1, vb1, (3, 21), all1)
    coarsen(
        functools.partial(l1.residual, vb1, g1), 2, tmp2, g2, (2, 10, lambda j: 2 * j), all1, 12
    )
    l2.first_sweep(g2, va2, (2, 10), all2)
    l2.sweep(va2, g2, vb2, (3, 9), all2)
    cells = [l2.residual(vb2, g2, 4 + i, 16, 16) for i in range(4)]
    for p, row in enumerate(pack_rows(cells)):
        yg[pl.ds(8 * (4 * parity + gy) + p, 1), :] = row
    yg_in = gather_near(yg, gather_sem.at[2], gather_sem.at[3])
    for x in range(4, 8):
        w2[0, x, pl.ds(16, 16), :] = vb2[x, pl.ds(16, 16), :]
        w2[1, x, pl.ds(16, 16), :] = g2[x, pl.ds(16, 16), :]
    w2_in = exchange(4, w2, w2, 4, 4, 4, 16, 8)
    arrive(xk_in)
    shape = (SLOTS, LANES)
    pack3, pack4 = Packed3(shape), Packed4(shape)
    kk = [xk[pl.ds(i, SLOTS, stride=8), :] for i in range(8)]
    f, d = packed_coefs(pack3, kk, 1.0 / 64)
    for i in range(8):
        for j, value in enumerate((f[0][i], f[1][i], f[2][i], OMEGA * recip(d[i]), d[i])):
            c3[j, i] = value
    l, t = grid2((LANES, LANES))

    def squeeze(values):
        out = None
        for i in range(4):
            y = t // 8 - 4 * i
            choose = jnp.where((l // 32 == y) & ((l % 16) // 2 == t % 8), 0.125, 0.0).astype(BF16)
            part = dot(values[2 * i] + values[2 * i + 1], choose)
            out = part if out is None else out + part
        return out

    f, d = packed_coefs(pack4, [squeeze(kk)], 1.0 / 256)
    weight = OMEGA * recip(d[0])
    faces4 = [weight]
    for axis, prv in enumerate((pack4.x_prev, pack4.y_prev, pack4.z_prev)):
        faces4 += [weight * f[axis][0], weight * prv(f[axis])[0]]
    for j, value in enumerate(faces4):
        c4[j] = value

    arrive(yg_in)
    assemble(yg, xg)
    xg_in = gather_x(xg, CHIPS, gather_sem.at[6], gather_sem.at[7])
    sent(1)
    arrive(xg_in)

    g3 = [xg[pl.ds(i, SLOTS, stride=8), :] for i in range(8)]
    f3 = [[c3[j, i] for i in range(8)] for j in range(3)]
    wt3 = [c3[3, i] for i in range(8)]
    saved = [a * b for a, b in zip(wt3, g3)]
    saved = packed_sweep(pack3, f3, wt3, saved, g3)
    around = pack3.both(f3, saved)
    g4 = squeeze([g3[i] + around[i] - c3[4, i] * saved[i] for i in range(8)])
    f4 = [c4[j] for j in range(7)]
    start = f4[0] * g4

    def coarsest(_, v):
        a = f4[1] * pack4.x_next([v])[0] + f4[2] * pack4.x_prev([v])[0]
        b = f4[3] * pack4.y_next([v])[0] + f4[4] * pack4.y_prev([v])[0]
        c = f4[5] * pack4.z_next([v])[0] + f4[6] * pack4.z_prev([v])[0]
        return ((1.0 - OMEGA) * v + start) + (a + b) + c

    v4 = lax.fori_loop(0, 7, coarsest, start)
    v = []
    for i in range(4):
        y = l // 8 - 4 * i
        spread = jnp.where((t // 32 == y) & ((t % 16) // 2 == l % 8), 1.0, 0.0).astype(BF16)
        part = dot(v4, spread)
        v += [saved[2 * i] + part, saved[2 * i + 1] + part]
    for _ in range(2):
        v = packed_sweep(pack3, f3, wt3, v, g3)
    for i in range(8):
        v3[i] = v[i]

    r, t8 = grid2((8, LANES))
    low = lax.rem(gy + (ngy - 1), ngy)
    high = lax.rem(gy + 1, ngy)
    parts = []
    for j in range(6):
        slot, p = 10 + j // 2, j % 2
        for part, y in ((low, 4), (gy, 0), (gy, 4), (high, 0)):
            rows = [v3[2 * part + p, pl.ds(slot + i, 1), :] for i in range(2)]
            row = jnp.broadcast_to(jnp.where(parity == 1, rows[0], rows[1]), (8, LANES))
            parts.append(jnp.where(t8 // 16 == r // 2 + y, row, 0.0))
    spread = jnp.where(l % 16 == t // 8, 1.0, 0.0).astype(BF16)
    fine = dot(jnp.concatenate(parts, axis=0), spread)
    for j in range(6):
        dup2[j] = fine[32 * j : 32 * j + 32]

    arrive(w2_in)

    def correct2(x):
        va2[x, pl.ds(8, 32), :] = w2[0, x, pl.ds(8, 32), :] + dup2[x // 2]

    loop(0, 12, correct2)
    l2.sweep(va2, w2.at[1], vb2, (1, 11), all2)
    l2.sweep(vb2, w2.at[1], va2, (2, 10), all2)

    def double2(x):
        c = va2[x, pl.ds(12, 24), :]
        dup1[x, pl.ds(8, 24, stride=2), :] = c
        dup1[x, pl.ds(9, 24, stride=2), :] = c

    loop(2, 10, double2)

    def correct1(x):
        for r, n in all1:
            va1[x, pl.ds(r, n), :] = vb1[x, pl.ds(r, n), :] + dup1[x // 2, pl.ds(r, n), :]

    loop(4, 20, correct1)
    l1.sweep(va1, g1, vb1, (5, 19), all1)
    l1.sweep(vb1, g1, va1, (6, 18), all1)

    def double1(x):
        c = va1[x, pl.ds(12, 40), :]
        tmp1[x, pl.ds(8, 40, stride=2), :] = c
        tmp1[x, pl.ds(9, 40, stride=2), :] = c

    loop(6, 18, double1)
    arrive(v0_in)

    def correct0(x):
        for r, n in all0:
            va0[x, pl.ds(r, n), :] = vs0[x, pl.ds(r, n), :] + tmp1[(x + 13) // 2, pl.ds(r, n), :]

    loop(0, 22, correct0)
    l0.sweep(va0, source, vb0, (1, 21), all0)
    l0.sweep(vb0, source, va0, (2, 20), all0)
    v_store = pltpu.make_async_copy(va0.at[pl.ds(3, 16), pl.ds(16, 64), :], v_out, store_sem.at[0])
    v_store.start()

    def final(x):
        for r, n in own0:
            res0[x - 3, pl.ds(r - 16, n), :] = l0.residual(va0, source, x, r, n)

    loop(3, 19, final)
    r_store = pltpu.make_async_copy(res0, r_out, store_sem.at[1])
    r_store.start()
    sent()
    v_store.wait()
    r_store.wait()


def solution(mesh):
    ngx, ngy = mesh.shape["gx"], mesh.shape["gy"]

    def vmem(*shape):
        return pltpu.VMEM(shape, F32)

    n0, n1, n2 = (22, 96, LANES), (24, 64, LANES), (12, 48, LANES)
    scratch = [vmem(3, *n0)] + [vmem(*n0)] * 9 + [vmem(16, 64, LANES)]
    scratch += [vmem(*n1)] * 10 + [vmem(12, 64, LANES)]
    scratch += [vmem(*n2)] * 10 + [vmem(2, *n2), vmem(6, 32, LANES)]
    scratch += [vmem(18, 96, LANES), vmem(12, 64, LANES), vmem(16, 96, LANES)]
    scratch += [vmem(64, LANES)] * 2 + [vmem(8 * SLOTS, LANES)] * 2
    scratch += [vmem(5, 8, SLOTS, LANES), vmem(7, SLOTS, LANES), vmem(8, SLOTS, LANES)]
    dma = pltpu.SemaphoreType.DMA
    scratch += [dma((3,)), dma((2,)), dma((7, 8)), dma((7, 8)), dma((8,))]

    def per_device(pressure, inverse_density, source):
        block = jax.ShapeDtypeStruct(pressure.shape, F32)
        return pl.pallas_call(
            functools.partial(kernel, ngx, ngy),
            out_shape=(block, block),
            in_specs=[pl.BlockSpec(memory_space=pltpu.HBM)] * 3,
            out_specs=[pl.BlockSpec(memory_space=pl.ANY)] * 2,
            scratch_shapes=scratch,
            compiler_params=pltpu.CompilerParams(
                collective_id=0, has_side_effects=True, vmem_limit_bytes=105 * 2**19
            ),
        )(pressure, inverse_density, source)

    spec = P("gx", "gy", None)
    return jax.shard_map(
        per_device, mesh=mesh, in_specs=(spec,) * 3, out_specs=(spec, spec), check_vma=False
    )
```

```python
import functools

import jax
import jax.numpy as jnp
from jax import lax
from jax.experimental import pallas as pl
from jax.experimental.pallas import tpu as pltpu
from jax.sharding import PartitionSpec as P

MESH = pl.DeviceIdType.MESH
F32 = jnp.float32
BF16 = jnp.bfloat16
OMEGA = 0.8
LANES = 128
SIDES = ((-1, 0), (1, 0), (0, -1), (0, 1), (-1, -1), (-1, 1), (1, -1), (1, 1))
SLOTS = 24
CHIPS = [c for d in range(5, 0, -1) for c in (d, -d)]


def recip(x):
    y = pl.reciprocal(x, approx=True)
    return y * (2.0 - x * y)


def roll(x, shift, axis):
    return pltpu.roll(x, shift % x.shape[axis], axis)


def loop(lo, hi, body):
    def step(i, carry):
        body(i)
        return carry

    lax.fori_loop(lo, hi, step, 0, unroll=hi - lo)


def strips(lo, hi, size=16):
    return [(r, min(size, hi - r)) for r in range(lo, hi, size)]


def lane_index(shape):
    return lax.broadcasted_iota(jnp.int32, shape, 1)


def pair_sum_z(x, s):
    first = (lane_index(x.shape) // s) % 2 == 0
    return x + jnp.where(first, roll(x, -s, 1), roll(x, s, 1))


class Level:
    def __init__(self, s, scale, k, r, fx, fy, fz, w, d):
        self.s, self.scale, self.k = s, scale, k
        self.r, self.fx, self.fy, self.fz, self.w, self.d = r, fx, fy, fz, w, d

    def inverses(self, planes, rows):
        def body(x):
            for r, n in rows:
                self.r[x, pl.ds(r, n), :] = (0.5 / self.scale) * recip(self.k[x, pl.ds(r, n), :])

        loop(*planes, body)

    def faces(self, planes, rows):
        def body(x):
            for r, n in rows:
                here = self.r[x, pl.ds(r, n), :]
                self.fx[x, pl.ds(r, n), :] = recip(here + self.r[x + 1, pl.ds(r, n), :])
                self.fy[x, pl.ds(r, n), :] = recip(here + self.r[x, pl.ds(r + 1, n), :])
                self.fz[x, pl.ds(r, n), :] = recip(here + roll(here, -self.s, 1))

        loop(*planes, body)

    def diagonal(self, planes, rows):
        def body(x):
            for r, n in rows:
                fz = self.fz[x, pl.ds(r, n), :]
                d = self.fx[x, pl.ds(r, n), :] + self.fx[x - 1, pl.ds(r, n), :]
                d += self.fy[x, pl.ds(r, n), :] + self.fy[x, pl.ds(r - 1, n), :]
                d += fz + roll(fz, self.s, 1)
                self.d[x, pl.ds(r, n), :] = d
                self.w[x, pl.ds(r, n), :] = OMEGA * recip(d)

        loop(*planes, body)

    def around(self, v, x, r, n):
        here = v[x, pl.ds(r, n), :]
        fz = self.fz[x, pl.ds(r, n), :]
        a = self.fx[x, pl.ds(r, n), :] * v[x + 1, pl.ds(r, n), :]
        a += self.fx[x - 1, pl.ds(r, n), :] * v[x - 1, pl.ds(r, n), :]
        a += self.fy[x, pl.ds(r, n), :] * v[x, pl.ds(r + 1, n), :]
        a += self.fy[x, pl.ds(r - 1, n), :] * v[x, pl.ds(r - 1, n), :]
        a += fz * roll(here, -self.s, 1) + roll(fz * here, self.s, 1)
        return here, a

    def first_sweep(self, g, dst, planes, rows):
        def body(x):
            for r, n in rows:
                dst[x, pl.ds(r, n), :] = self.w[x, pl.ds(r, n), :] * g[x, pl.ds(r, n), :]

        loop(*planes, body)

    def sweep(self, src, g, dst, planes, rows):
        def body(x):
            for r, n in rows:
                here, a = self.around(src, x, r, n)
                w = self.w[x, pl.ds(r, n), :]
                dst[x, pl.ds(r, n), :] = (1.0 - OMEGA) * here + w * (g[x, pl.ds(r, n), :] + a)

        loop(*planes, body)

    def residual(self, v, g, x, r, n):
        here, a = self.around(v, x, r, n)
        return g[x, pl.ds(r, n), :] + a - self.d[x, pl.ds(r, n), :] * here


def add_planes(value, tmp, pairs, rows):
    lo, hi, plane = pairs

    def gather(j):
        x = plane(j)
        for r, n in rows:
            tmp[j, pl.ds(r, n), :] = value(x, r, n) + value(x + 1, r, n)

    loop(lo, hi, gather)


def coarsen(value, s, tmp, dst, pairs, rows, dst_rows, parts=None):
    lo, hi, plane = pairs
    for part_lo, part_hi, part_rows in parts or [(lo, hi, rows)]:
        add_planes(value, tmp, (part_lo, part_hi, plane), part_rows)
    first, count = rows[0][0], sum(n for _, n in rows) // 2

    def squeeze(j):
        even = tmp[j, pl.ds(first, count, stride=2), :]
        odd = tmp[j, pl.ds(first + 1, count, stride=2), :]
        dst[j, pl.ds(dst_rows, count), :] = 0.125 * pair_sum_z(even + odd, s)

    loop(lo, hi, squeeze)


class Packed3:
    def __init__(self, shape):
        lane = lane_index(shape)
        self.y_last, self.y_first = lane >= 112, lane < 16
        self.z_last, self.z_first = lane % 16 == 15, lane % 16 == 0

    def y_next(self, v):
        t = [roll(a, -16, 1) for a in v]
        return [jnp.where(self.y_last, t[(i + 2) % 8], t[i]) for i in range(8)]

    def y_prev(self, v):
        t = [roll(a, 16, 1) for a in v]
        return [jnp.where(self.y_first, t[(i - 2) % 8], t[i]) for i in range(8)]

    def z_next(self, v):
        return [jnp.where(self.z_last, roll(a, 15, 1), roll(a, -1, 1)) for a in v]

    def z_prev(self, v):
        return [jnp.where(self.z_first, roll(a, -15, 1), roll(a, 1, 1)) for a in v]

    def x_next(self, v):
        return [v[i + 1] if i % 2 == 0 else roll(v[i - 1], -1, 0) for i in range(8)]

    def x_prev(self, v):
        return [roll(v[i + 1], 1, 0) if i % 2 == 0 else v[i - 1] for i in range(8)]

    def both(self, f, v):
        out = None
        for axis in range(3):
            nxt = (self.x_next, self.y_next, self.z_next)[axis](v)
            prv = (self.x_prev, self.y_prev, self.z_prev)[axis]([a * b for a, b in zip(f[axis], v)])
            term = [a * b + c for a, b, c in zip(f[axis], nxt, prv)]
            out = term if out is None else [a + b for a, b in zip(out, term)]
        return out


class Packed4(Packed3):
    def __init__(self, shape):
        lane = lane_index(shape)
        self.z_last, self.z_first = lane % 8 == 7, lane % 8 == 0

    def y_next(self, v):
        return [roll(v[0], -8, 1)]

    def y_prev(self, v):
        return [roll(v[0], 8, 1)]

    def z_next(self, v):
        return [jnp.where(self.z_last, roll(v[0], 7, 1), roll(v[0], -1, 1))]

    def z_prev(self, v):
        return [jnp.where(self.z_first, roll(v[0], -7, 1), roll(v[0], 1, 1))]

    def x_next(self, v):
        return [roll(v[0], -1, 0)]

    def x_prev(self, v):
        return [roll(v[0], 1, 0)]


def packed_coefs(pack, k, scale):
    r = [(0.5 / scale) * recip(a) for a in k]
    f = []
    d = None
    for nxt, prv in ((pack.x_next, pack.x_prev), (pack.y_next, pack.y_prev), (pack.z_next, pack.z_prev)):
        face = [recip(a + b) for a, b in zip(r, nxt(r))]
        f.append(face)
        both = [a + b for a, b in zip(face, prv(face))]
        d = both if d is None else [a + b for a, b in zip(d, both)]
    return f, d


def packed_sweep(pack, f, w, v, g):
    return [
        (1.0 - OMEGA) * a + b * (c + e) for a, b, c, e in zip(v, w, g, pack.both(f, v))
    ]


def dot(a, choose):
    out = None
    for _ in range(3):
        part = a.astype(BF16)
        a = a - part.astype(F32)
        term = jnp.dot(part, choose, preferred_element_type=F32)
        out = term if out is None else out + term
    return out


def grid2(shape):
    return lax.broadcasted_iota(jnp.int32, shape, 0), lax.broadcasted_iota(jnp.int32, shape, 1)


def pack_rows(cells):
    l, t = grid2((LANES, LANES))
    choose = jnp.where((l // 8 == t % 16) & (l % 4 == 0), 0.125, 0.0).astype(BF16)
    r, t = grid2((16, LANES))
    keep = r // 2 == t // 16
    rows = []
    for p in range(2):
        u = dot(cells[2 * p] + cells[2 * p + 1], choose)
        rows.append(jnp.sum(jnp.where(keep, u, 0.0), axis=0, keepdims=True))
    return rows


def kernel(
    ngx, ngy, p_hbm, k_hbm, s_hbm, v_out, r_out,
    w0, r0, fx0, fy0, fz0, wt0, d0, va0, vb0, vs0, res0,
    k1, r1, fx1, fy1, fz1, wt1, d1, g1, va1, vb1, dup1,
    k2, r2, fx2, fy2, fz2, wt2, d2, g2, va2, vb2, w2, dup2,
    tmp1, tmp2, tmp0, yk, yg, xk, xg, c3, c4, v3,
    load_sem, store_sem, side_s, side_r, gather_sem,
):
    gx, gy = lax.axis_index("gx"), lax.axis_index("gy")
    parity = lax.rem(gx, 2)

    def peer(dx, dy):
        return (lax.rem(gx + (dx + ngx), ngx), lax.rem(gy + (dy + ngy), ngy))

    loads = [
        pltpu.make_async_copy(hbm, w0.at[i, pl.ds(3, 16), pl.ds(16, 64), :], load_sem.at[i])
        for i, hbm in ((1, k_hbm), (0, p_hbm), (2, s_hbm))
    ]
    for c in loads:
        c.start()

    greet = [(2 * c, 0) for c in (6, -6, *CHIPS)] + [(0, 2), (1 - 2 * parity, 2)] + list(SIDES)[::-1]
    barrier = pltpu.get_barrier_semaphore()
    for o in greet:
        pl.semaphore_signal(barrier, inc=1, device_id=peer(*o), device_id_type=MESH)

    waits = []

    def exchange(which, src, dst, x0, nx, hx, ny, hy):
        y0 = 16
        lead = (slice(None),) * (len(src.shape) - 3)
        copies = []
        for i, (dx, dy) in enumerate(SIDES):
            xs, xd, xn = ((x0, x0 + nx, hx), (x0, x0, nx), (x0 + nx - hx, x0 - hx, hx))[dx + 1]
            ys, yd, yn = ((y0, y0 + ny, hy), (y0, y0, ny), (y0 + ny - hy, y0 - hy, hy))[dy + 1]
            c = pltpu.make_async_remote_copy(
                src_ref=src.at[lead + (pl.ds(xs, xn), pl.ds(ys, yn))],
                dst_ref=dst.at[lead + (pl.ds(xd, xn), pl.ds(yd, yn))],
                send_sem=side_s.at[which, i], recv_sem=side_r.at[which, i],
                device_id=peer(dx, dy), device_id_type=MESH,
            )
            c.start()
            copies.append(c)
        waits.extend(copies)
        return copies

    def wait_all(buf, tiles, send, recv):
        every = buf.at[pl.ds(0, 8 * tiles), :]
        c = pltpu.make_async_remote_copy(
            src_ref=every, dst_ref=every, send_sem=send, recv_sem=recv,
            device_id=peer(1, 0), device_id_type=MESH,
        )
        waits.append(c)
        return [c]

    def gather_near(buf, send, recv):
        mine = pl.ds(pl.multiple_of(8 * (4 * parity + gy), 8), 8)
        for dx, dy in ((1, 2), (0, 2), (1, 1), (1, 3), (0, 1), (0, 3), (1, 0)):
            c = pltpu.make_async_remote_copy(
                src_ref=buf.at[mine, :], dst_ref=buf.at[mine, :], send_sem=send, recv_sem=recv,
                device_id=peer(dx * (1 - 2 * parity), dy), device_id_type=MESH,
            )
            c.start()
        return wait_all(buf, 7, send, recv)

    def chip_rows(c):
        return pl.ds(pl.multiple_of(16 * (6 + c - parity), 16), 16)

    def gather_x(buf, chips, send, recv):
        for c in chips:
            copy = pltpu.make_async_remote_copy(
                src_ref=buf.at[chip_rows(0), :], dst_ref=buf.at[chip_rows(-c), :], send_sem=send, recv_sem=recv,
                device_id=peer(2 * c, 0), device_id_type=MESH,
            )
            copy.start()
        return wait_all(buf, 2 * len(chips), send, recv)

    def assemble(near, buf):
        for device in range(2):
            for i in range(4):
                row = pl.multiple_of(8 * (2 * (6 - parity) + device), 8) + 2 * i
                buf[pl.ds(row, 2), :] = near[pl.ds(8 * (4 * device + i), 2), :]

    def arrive(copies):
        for c in copies:
            c.wait_recv()

    def sent(keep=0):
        count = len(waits) - keep
        for c in waits[:count]:
            c.wait_send()
        del waits[:count]

    press, coef, source = w0.at[0], w0.at[1], w0.at[2]
    l0 = Level(1, 1.0, coef, r0, fx0, fy0, fz0, wt0, d0)
    l1 = Level(2, 0.25, k1, r1, fx1, fy1, fz1, wt1, d1)
    l2 = Level(4, 0.0625, k2, r2, fx2, fy2, fz2, wt2, d2)
    all0, own0, mid0, rim0 = strips(8, 88), strips(16, 80), strips(24, 72), [(8, 16), (72, 16)]
    all1, own1 = strips(8, 56), strips(16, 48)
    all2 = strips(8, 40)

    for c in loads:
        c.wait()
    pl.semaphore_wait(barrier, len(greet))
    coef_in = exchange(0, coef, coef, 3, 16, 3, 64, 3)
    press_in = exchange(5, press, press, 3, 16, 3, 64, 3)
    source_in = exchange(6, source, source, 3, 16, 2, 64, 2)
    coarsen(lambda x, r, n: coef[x, pl.ds(r, n), :], 1, tmp1, k1, (8, 16, lambda j: 2 * j - 13), own0, 16)
    coarsen(lambda x, r, n: k1[x, pl.ds(r, n), :], 2, tmp2, k2, (4, 8, lambda j: 2 * j), own1, 16)
    for p, row in enumerate(pack_rows([k2[4 + i, pl.ds(16, 16), :] for i in range(4)])):
        yk[pl.ds(8 * (4 * parity + gy) + p, 1), :] = row
    k1_in = exchange(1, k1, k1, 8, 8, 8, 32, 8)
    yk_in = gather_near(yk, gather_sem.at[0], gather_sem.at[1])

    l0.inverses((3, 19), own0)
    l0.faces((3, 18), own0)
    l0.diagonal((4, 18), own0)
    l0.sweep(press, source, va0, (4, 18), [(17, 7), *mid0, (72, 7)])
    l0.sweep(va0, source, vb0, (5, 17), mid0)
    residual0 = functools.partial(l0.residual, vb0, source)
    add_planes(residual0, tmp0, (10, 14, lambda j: 2 * j - 13), strips(32, 64))

    arrive(coef_in)
    for planes in ((0, 3), (19, 22)):
        l0.inverses(planes, all0)
    l0.inverses((3, 19), [(8, 8), (80, 8)])
    for planes in ((0, 3), (18, 21)):
        l0.faces(planes, all0)
    l0.faces((3, 18), [(8, 8), (72, 16)])
    for planes in ((1, 4), (18, 21)):
        l0.diagonal(planes, all0)
    l0.diagonal((4, 18), rim0)
    arrive(press_in)
    arrive(source_in)
    for planes in ((1, 4), (18, 21)):
        l0.sweep(press, source, va0, planes, all0)
    l0.sweep(press, source, va0, (4, 18), rim0)
    for planes in ((2, 5), (17, 20)):
        l0.sweep(va0, source, vb0, planes, all0)
    l0.sweep(va0, source, vb0, (5, 17), rim0)
    edge0 = [(16, 16), (64, 16)]
    coarsen(
        residual0, 1, tmp0, g1, (8, 16, lambda j: 2 * j - 13), own0, 16,
        [(8, 10, own0), (10, 14, edge0), (14, 16, own0)],
    )
    g1_in = exchange(2, g1, g1, 8, 8, 6, 32, 8)
    arrive(yk_in)
    assemble(yk, xk)
    xk_in = gather_x(xk, [6 - 12 * parity, *CHIPS], gather_sem.at[4], gather_sem.at[5])

    arrive(k1_in)
    l1.inverses((0, 24), all1)
    l1.faces((0, 23), all1)
    l1.diagonal((1, 23), all1)
    coarsen(lambda x, r, n: k1[x, pl.ds(r, n), :], 2, tmp2, k2, (0, 12, lambda j: 2 * j), strips(0, 64), 8)
    l2.inverses((0, 12), all2)
    l2.faces((0, 11), all2)
    l2.diagonal((1, 11), all2)

    def keep(x):
        for r, n in own0:
            vs0[x, pl.ds(r, n), :] = vb0[x, pl.ds(r, n), :]

    loop(3, 19, keep)

    arrive(g1_in)
    v0_in = exchange(3, vb0, vs0, 3, 16, 3, 64, 3)
    l1.first_sweep(g1, va1, (2, 22), all1)
    l1.sweep(va1, g1, vb1, (3, 21), all1)
    coarsen(
        functools.partial(l1.residual, vb1, g1), 2, tmp2, g2, (2, 10, lambda j: 2 * j), all1, 12
    )
    l2.first_sweep(g2, va2, (2, 10), all2)
    l2.sweep(va2, g2, vb2, (3, 9), all2)
    cells = [l2.residual(vb2, g2, 4 + i, 16, 16) for i in range(4)]
    for p, row in enumerate(pack_rows(cells)):
        yg[pl.ds(8 * (4 * parity + gy) + p, 1), :] = row
    yg_in = gather_near(yg, gather_sem.at[2], gather_sem.at[3])
    for x in range(4, 8):
        w2[0, x, pl.ds(16, 16), :] = vb2[x, pl.ds(16, 16), :]
        w2[1, x, pl.ds(16, 16), :] = g2[x, pl.ds(16, 16), :]
    w2_in = exchange(4, w2, w2, 4, 4, 4, 16, 8)
    arrive(xk_in)
    shape = (SLOTS, LANES)
    pack3, pack4 = Packed3(shape), Packed4(shape)
    kk = [xk[pl.ds(i, SLOTS, stride=8), :] for i in range(8)]
    f, d = packed_coefs(pack3, kk, 1.0 / 64)
    for i in range(8):
        for j, value in enumerate((f[0][i], f[1][i], f[2][i], OMEGA * recip(d[i]), d[i])):
            c3[j, i] = value
    l, t = grid2((LANES, LANES))

    def squeeze(values):
        out = None
        for i in range(4):
            y = t // 8 - 4 * i
            choose = jnp.where((l // 32 == y) & ((l % 16) // 2 == t % 8), 0.125, 0.0).astype(BF16)
            part = dot(values[2 * i] + values[2 * i + 1], choose)
            out = part if out is None else out + part
        return out

    f, d = packed_coefs(pack4, [squeeze(kk)], 1.0 / 256)
    weight = OMEGA * recip(d[0])
    faces4 = [weight]
    for axis, prv in enumerate((pack4.x_prev, pack4.y_prev, pack4.z_prev)):
        faces4 += [weight * f[axis][0], weight * prv(f[axis])[0]]
    for j, value in enumerate(faces4):
        c4[j] = value

    arrive(yg_in)
    assemble(yg, xg)
    xg_in = gather_x(xg, CHIPS, gather_sem.at[6], gather_sem.at[7])
    sent(1)
    arrive(xg_in)

    g3 = [xg[pl.ds(i, SLOTS, stride=8), :] for i in range(8)]
    f3 = [[c3[j, i] for i in range(8)] for j in range(3)]
    wt3 = [c3[3, i] for i in range(8)]
    saved = [a * b for a, b in zip(wt3, g3)]
    saved = packed_sweep(pack3, f3, wt3, saved, g3)
    around = pack3.both(f3, saved)
    g4 = squeeze([g3[i] + around[i] - c3[4, i] * saved[i] for i in range(8)])
    f4 = [c4[j] for j in range(7)]
    start = f4[0] * g4

    def coarsest(_, v):
        a = f4[1] * pack4.x_next([v])[0] + f4[2] * pack4.x_prev([v])[0]
        b = f4[3] * pack4.y_next([v])[0] + f4[4] * pack4.y_prev([v])[0]
        c = f4[5] * pack4.z_next([v])[0] + f4[6] * pack4.z_prev([v])[0]
        return ((1.0 - OMEGA) * v + start) + (a + b) + c

    v4 = lax.fori_loop(0, 7, coarsest, start)
    v = []
    for i in range(4):
        y = l // 8 - 4 * i
        spread = jnp.where((t // 32 == y) & ((t % 16) // 2 == l % 8), 1.0, 0.0).astype(BF16)
        part = dot(v4, spread)
        v += [saved[2 * i] + part, saved[2 * i + 1] + part]
    for _ in range(2):
        v = packed_sweep(pack3, f3, wt3, v, g3)
    for i in range(8):
        v3[i] = v[i]

    r, t8 = grid2((8, LANES))
    low = lax.rem(gy + (ngy - 1), ngy)
    high = lax.rem(gy + 1, ngy)
    parts = []
    for j in range(6):
        slot, p = 10 + j // 2, j % 2
        for part, y in ((low, 4), (gy, 0), (gy, 4), (high, 0)):
            rows = [v3[2 * part + p, pl.ds(slot + i, 1), :] for i in range(2)]
            row = jnp.broadcast_to(jnp.where(parity == 1, rows[0], rows[1]), (8, LANES))
            parts.append(jnp.where(t8 // 16 == r // 2 + y, row, 0.0))
    spread = jnp.where(l % 16 == t // 8, 1.0, 0.0).astype(BF16)
    fine = dot(jnp.concatenate(parts, axis=0), spread)
    for j in range(6):
        dup2[j] = fine[32 * j : 32 * j + 32]

    arrive(w2_in)

    def correct2(x):
        va2[x, pl.ds(8, 32), :] = w2[0, x, pl.ds(8, 32), :] + dup2[x // 2]

    loop(0, 12, correct2)
    l2.sweep(va2, w2.at[1], vb2, (1, 11), all2)
    l2.sweep(vb2, w2.at[1], va2, (2, 10), all2)

    def double2(x):
        c = va2[x, pl.ds(12, 24), :]
        dup1[x, pl.ds(8, 24, stride=2), :] = c
        dup1[x, pl.ds(9, 24, stride=2), :] = c

    loop(2, 10, double2)

    def correct1(x):
        for r, n in all1:
            va1[x, pl.ds(r, n), :] = vb1[x, pl.ds(r, n), :] + dup1[x // 2, pl.ds(r, n), :]

    loop(4, 20, correct1)
    l1.sweep(va1, g1, vb1, (5, 19), all1)
    l1.sweep(vb1, g1, va1, (6, 18), all1)

    def double1(x):
        c = va1[x, pl.ds(12, 40), :]
        tmp1[x, pl.ds(8, 40, stride=2), :] = c
        tmp1[x, pl.ds(9, 40, stride=2), :] = c

    loop(6, 18, double1)
    arrive(v0_in)

    def correct0(x):
        for r, n in all0:
            va0[x, pl.ds(r, n), :] = vs0[x, pl.ds(r, n), :] + tmp1[(x + 13) // 2, pl.ds(r, n), :]

    loop(0, 22, correct0)
    l0.sweep(va0, source, vb0, (1, 21), all0)
    l0.sweep(vb0, source, va0, (2, 20), all0)
    v_store = pltpu.make_async_copy(va0.at[pl.ds(3, 16), pl.ds(16, 64), :], v_out, store_sem.at[0])
    v_store.start()

    def final(x):
        for r, n in own0:
            res0[x - 3, pl.ds(r - 16, n), :] = l0.residual(va0, source, x, r, n)

    stores = [v_store]
    for half in range(2):
        loop(3 + 8 * half, 11 + 8 * half, final)
        planes = pl.ds(8 * half, 8)
        stores.append(pltpu.make_async_copy(res0.at[planes], r_out.at[planes], store_sem.at[1 + half]))
        stores[-1].start()
    sent()
    for c in stores:
        c.wait()


def solution(mesh):
    ngx, ngy = mesh.shape["gx"], mesh.shape["gy"]

    def vmem(*shape):
        return pltpu.VMEM(shape, F32)

    n0, n1, n2 = (22, 96, LANES), (24, 64, LANES), (12, 48, LANES)
    scratch = [vmem(3, *n0)] + [vmem(*n0)] * 9 + [vmem(16, 64, LANES)]
    scratch += [vmem(*n1)] * 10 + [vmem(12, 64, LANES)]
    scratch += [vmem(*n2)] * 10 + [vmem(2, *n2), vmem(6, 32, LANES)]
    scratch += [vmem(18, 96, LANES), vmem(12, 64, LANES), vmem(16, 96, LANES)]
    scratch += [vmem(64, LANES)] * 2 + [vmem(8 * SLOTS, LANES)] * 2
    scratch += [vmem(5, 8, SLOTS, LANES), vmem(7, SLOTS, LANES), vmem(8, SLOTS, LANES)]
    dma = pltpu.SemaphoreType.DMA
    scratch += [dma((3,)), dma((3,)), dma((7, 8)), dma((7, 8)), dma((8,))]

    def per_device(pressure, inverse_density, source):
        block = jax.ShapeDtypeStruct(pressure.shape, F32)
        return pl.pallas_call(
            functools.partial(kernel, ngx, ngy),
            out_shape=(block, block),
            in_specs=[pl.BlockSpec(memory_space=pltpu.HBM)] * 3,
            out_specs=[pl.BlockSpec(memory_space=pl.ANY)] * 2,
            scratch_shapes=scratch,
            compiler_params=pltpu.CompilerParams(
                collective_id=0, has_side_effects=True, vmem_limit_bytes=105 * 2**19
            ),
        )(pressure, inverse_density, source)

    spec = P("gx", "gy", None)
    return jax.shard_map(
        per_device, mesh=mesh, in_specs=(spec,) * 3, out_specs=(spec, spec), check_vma=False
    )
```

```python
import functools

import jax
import jax.numpy as jnp
from jax import lax
from jax.experimental import pallas as pl
from jax.experimental.pallas import tpu as pltpu
from jax.sharding import PartitionSpec as P

MESH = pl.DeviceIdType.MESH
F32 = jnp.float32
BF16 = jnp.bfloat16
OMEGA = 0.8
LANES = 128
SIDES = ((-1, 0), (1, 0), (0, -1), (0, 1), (-1, -1), (-1, 1), (1, -1), (1, 1))
SLOTS = 24
CHIPS = [c for d in range(5, 0, -1) for c in (d, -d)]


def recip(x):
    y = pl.reciprocal(x, approx=True)
    return y * (2.0 - x * y)


def roll(x, shift, axis):
    return pltpu.roll(x, shift % x.shape[axis], axis)


def loop(lo, hi, body):
    def step(i, carry):
        body(i)
        return carry

    lax.fori_loop(lo, hi, step, 0, unroll=hi - lo)


def strips(lo, hi, size=16):
    return [(r, min(size, hi - r)) for r in range(lo, hi, size)]


def lane_index(shape):
    return lax.broadcasted_iota(jnp.int32, shape, 1)


def pair_sum_z(x, s):
    first = (lane_index(x.shape) // s) % 2 == 0
    return x + jnp.where(first, roll(x, -s, 1), roll(x, s, 1))


class Level:
    def __init__(self, s, scale, k, r, fx, fy, fz, w, d):
        self.s, self.scale, self.k = s, scale, k
        self.r, self.fx, self.fy, self.fz, self.w, self.d = r, fx, fy, fz, w, d

    def inverses(self, planes, rows):
        def body(x):
            for r, n in rows:
                self.r[x, pl.ds(r, n), :] = (0.5 / self.scale) * recip(self.k[x, pl.ds(r, n), :])

        loop(*planes, body)

    def faces(self, planes, rows):
        def body(x):
            for r, n in rows:
                here = self.r[x, pl.ds(r, n), :]
                self.fx[x, pl.ds(r, n), :] = recip(here + self.r[x + 1, pl.ds(r, n), :])
                self.fy[x, pl.ds(r, n), :] = recip(here + self.r[x, pl.ds(r + 1, n), :])
                self.fz[x, pl.ds(r, n), :] = recip(here + roll(here, -self.s, 1))

        loop(*planes, body)

    def diagonal(self, planes, rows):
        def body(x):
            for r, n in rows:
                fz = self.fz[x, pl.ds(r, n), :]
                d = self.fx[x, pl.ds(r, n), :] + self.fx[x - 1, pl.ds(r, n), :]
                d += self.fy[x, pl.ds(r, n), :] + self.fy[x, pl.ds(r - 1, n), :]
                d += fz + roll(fz, self.s, 1)
                self.d[x, pl.ds(r, n), :] = d
                self.w[x, pl.ds(r, n), :] = OMEGA * recip(d)

        loop(*planes, body)

    def around(self, v, x, r, n):
        here = v[x, pl.ds(r, n), :]
        fz = self.fz[x, pl.ds(r, n), :]
        a = self.fx[x, pl.ds(r, n), :] * v[x + 1, pl.ds(r, n), :]
        a += self.fx[x - 1, pl.ds(r, n), :] * v[x - 1, pl.ds(r, n), :]
        a += self.fy[x, pl.ds(r, n), :] * v[x, pl.ds(r + 1, n), :]
        a += self.fy[x, pl.ds(r - 1, n), :] * v[x, pl.ds(r - 1, n), :]
        a += fz * roll(here, -self.s, 1) + roll(fz * here, self.s, 1)
        return here, a

    def first_sweep(self, g, dst, planes, rows):
        def body(x):
            for r, n in rows:
                dst[x, pl.ds(r, n), :] = self.w[x, pl.ds(r, n), :] * g[x, pl.ds(r, n), :]

        loop(*planes, body)

    def sweep(self, src, g, dst, planes, rows):
        def body(x):
            for r, n in rows:
                here, a = self.around(src, x, r, n)
                w = self.w[x, pl.ds(r, n), :]
                dst[x, pl.ds(r, n), :] = (1.0 - OMEGA) * here + w * (g[x, pl.ds(r, n), :] + a)

        loop(*planes, body)

    def residual(self, v, g, x, r, n):
        here, a = self.around(v, x, r, n)
        return g[x, pl.ds(r, n), :] + a - self.d[x, pl.ds(r, n), :] * here


def add_planes(value, tmp, pairs, rows):
    lo, hi, plane = pairs

    def gather(j):
        x = plane(j)
        for r, n in rows:
            tmp[j, pl.ds(r, n), :] = value(x, r, n) + value(x + 1, r, n)

    loop(lo, hi, gather)


def coarsen(value, s, tmp, dst, pairs, rows, dst_rows, parts=None):
    lo, hi, plane = pairs
    for part_lo, part_hi, part_rows in parts or [(lo, hi, rows)]:
        add_planes(value, tmp, (part_lo, part_hi, plane), part_rows)
    first, count = rows[0][0], sum(n for _, n in rows) // 2

    def squeeze(j):
        even = tmp[j, pl.ds(first, count, stride=2), :]
        odd = tmp[j, pl.ds(first + 1, count, stride=2), :]
        dst[j, pl.ds(dst_rows, count), :] = 0.125 * pair_sum_z(even + odd, s)

    loop(lo, hi, squeeze)


class Packed3:
    def __init__(self, shape):
        lane = lane_index(shape)
        self.y_last, self.y_first = lane >= 112, lane < 16
        self.z_last, self.z_first = lane % 16 == 15, lane % 16 == 0

    def y_next(self, v):
        t = [roll(a, -16, 1) for a in v]
        return [jnp.where(self.y_last, t[(i + 2) % 8], t[i]) for i in range(8)]

    def y_prev(self, v):
        t = [roll(a, 16, 1) for a in v]
        return [jnp.where(self.y_first, t[(i - 2) % 8], t[i]) for i in range(8)]

    def z_next(self, v):
        return [jnp.where(self.z_last, roll(a, 15, 1), roll(a, -1, 1)) for a in v]

    def z_prev(self, v):
        return [jnp.where(self.z_first, roll(a, -15, 1), roll(a, 1, 1)) for a in v]

    def x_next(self, v):
        return [v[i + 1] if i % 2 == 0 else roll(v[i - 1], -1, 0) for i in range(8)]

    def x_prev(self, v):
        return [roll(v[i + 1], 1, 0) if i % 2 == 0 else v[i - 1] for i in range(8)]

    def both(self, f, v):
        out = None
        for axis in range(3):
            nxt = (self.x_next, self.y_next, self.z_next)[axis](v)
            prv = (self.x_prev, self.y_prev, self.z_prev)[axis]([a * b for a, b in zip(f[axis], v)])
            term = [a * b + c for a, b, c in zip(f[axis], nxt, prv)]
            out = term if out is None else [a + b for a, b in zip(out, term)]
        return out


class Packed4(Packed3):
    def __init__(self, shape):
        lane = lane_index(shape)
        self.z_last, self.z_first = lane % 8 == 7, lane % 8 == 0

    def y_next(self, v):
        return [roll(v[0], -8, 1)]

    def y_prev(self, v):
        return [roll(v[0], 8, 1)]

    def z_next(self, v):
        return [jnp.where(self.z_last, roll(v[0], 7, 1), roll(v[0], -1, 1))]

    def z_prev(self, v):
        return [jnp.where(self.z_first, roll(v[0], -7, 1), roll(v[0], 1, 1))]

    def x_next(self, v):
        return [roll(v[0], -1, 0)]

    def x_prev(self, v):
        return [roll(v[0], 1, 0)]


def packed_coefs(pack, k, scale):
    r = [(0.5 / scale) * recip(a) for a in k]
    f = []
    d = None
    for nxt, prv in ((pack.x_next, pack.x_prev), (pack.y_next, pack.y_prev), (pack.z_next, pack.z_prev)):
        face = [recip(a + b) for a, b in zip(r, nxt(r))]
        f.append(face)
        both = [a + b for a, b in zip(face, prv(face))]
        d = both if d is None else [a + b for a, b in zip(d, both)]
    return f, d


def packed_sweep(pack, f, w, v, g):
    return [
        (1.0 - OMEGA) * a + b * (c + e) for a, b, c, e in zip(v, w, g, pack.both(f, v))
    ]


def dot(a, choose):
    out = None
    for _ in range(3):
        part = a.astype(BF16)
        a = a - part.astype(F32)
        term = jnp.dot(part, choose, preferred_element_type=F32)
        out = term if out is None else out + term
    return out


def grid2(shape):
    return lax.broadcasted_iota(jnp.int32, shape, 0), lax.broadcasted_iota(jnp.int32, shape, 1)


def pack_rows(cells):
    l, t = grid2((LANES, LANES))
    choose = jnp.where((l // 8 == t % 16) & (l % 4 == 0), 0.125, 0.0).astype(BF16)
    r, t = grid2((16, LANES))
    keep = r // 2 == t // 16
    rows = []
    for p in range(2):
        u = dot(cells[2 * p] + cells[2 * p + 1], choose)
        rows.append(jnp.sum(jnp.where(keep, u, 0.0), axis=0, keepdims=True))
    return rows


def kernel(
    ngx, ngy, p_hbm, k_hbm, s_hbm, v_out, r_out,
    w0, r0, fx0, fy0, fz0, wt0, d0, va0, vb0, vs0, res0,
    k1, r1, fx1, fy1, fz1, wt1, d1, g1, va1, vb1, dup1, pk1,
    k2, r2, fx2, fy2, fz2, wt2, d2, g2, va2, vb2, w2, dup2,
    tmp1, tmp2, tmp0, yk, yg, xk, xg, c3, c4, v3,
    load_sem, store_sem, side_s, side_r, gather_sem,
):
    gx, gy = lax.axis_index("gx"), lax.axis_index("gy")
    parity = lax.rem(gx, 2)

    def peer(dx, dy):
        return (lax.rem(gx + (dx + ngx), ngx), lax.rem(gy + (dy + ngy), ngy))

    loads = [
        pltpu.make_async_copy(hbm, w0.at[i, pl.ds(3, 16), pl.ds(16, 64), :], load_sem.at[i])
        for i, hbm in ((1, k_hbm), (0, p_hbm), (2, s_hbm))
    ]
    for c in loads:
        c.start()

    greet = [(2 * c, 0) for c in (6, -6, *CHIPS)] + [(0, 2), (1 - 2 * parity, 2)] + list(SIDES)[::-1]
    barrier = pltpu.get_barrier_semaphore()
    for o in greet:
        pl.semaphore_signal(barrier, inc=1, device_id=peer(*o), device_id_type=MESH)

    waits = []

    def exchange(which, src, dst, x0, nx, hx, ny, hy):
        y0 = 16
        lead = (slice(None),) * (len(src.shape) - 3)
        copies = []
        for i, (dx, dy) in enumerate(SIDES):
            xs, xd, xn = ((x0, x0 + nx, hx), (x0, x0, nx), (x0 + nx - hx, x0 - hx, hx))[dx + 1]
            ys, yd, yn = ((y0, y0 + ny, hy), (y0, y0, ny), (y0 + ny - hy, y0 - hy, hy))[dy + 1]
            c = pltpu.make_async_remote_copy(
                src_ref=src.at[lead + (pl.ds(xs, xn), pl.ds(ys, yn))],
                dst_ref=dst.at[lead + (pl.ds(xd, xn), pl.ds(yd, yn))],
                send_sem=side_s.at[which, i], recv_sem=side_r.at[which, i],
                device_id=peer(dx, dy), device_id_type=MESH,
            )
            c.start()
            copies.append(c)
        waits.extend(copies)
        return copies

    def wait_all(buf, tiles, send, recv):
        every = buf.at[pl.ds(0, 8 * tiles), :]
        c = pltpu.make_async_remote_copy(
            src_ref=every, dst_ref=every, send_sem=send, recv_sem=recv,
            device_id=peer(1, 0), device_id_type=MESH,
        )
        waits.append(c)
        return [c]

    def gather_near(buf, send, recv):
        mine = pl.ds(pl.multiple_of(8 * (4 * parity + gy), 8), 8)
        for dx, dy in ((1, 2), (0, 2), (1, 1), (1, 3), (0, 1), (0, 3), (1, 0)):
            c = pltpu.make_async_remote_copy(
                src_ref=buf.at[mine, :], dst_ref=buf.at[mine, :], send_sem=send, recv_sem=recv,
                device_id=peer(dx * (1 - 2 * parity), dy), device_id_type=MESH,
            )
            c.start()
        return wait_all(buf, 7, send, recv)

    def chip_rows(c):
        return pl.ds(pl.multiple_of(16 * (6 + c - parity), 16), 16)

    def gather_x(buf, chips, send, recv):
        for c in chips:
            copy = pltpu.make_async_remote_copy(
                src_ref=buf.at[chip_rows(0), :], dst_ref=buf.at[chip_rows(-c), :], send_sem=send, recv_sem=recv,
                device_id=peer(2 * c, 0), device_id_type=MESH,
            )
            copy.start()
        return wait_all(buf, 2 * len(chips), send, recv)

    def assemble(near, buf):
        for device in range(2):
            for i in range(4):
                row = pl.multiple_of(8 * (2 * (6 - parity) + device), 8) + 2 * i
                buf[pl.ds(row, 2), :] = near[pl.ds(8 * (4 * device + i), 2), :]

    def arrive(copies):
        for c in copies:
            c.wait_recv()

    def sent(keep=0):
        count = len(waits) - keep
        for c in waits[:count]:
            c.wait_send()
        del waits[:count]

    press, coef, source = w0.at[0], w0.at[1], w0.at[2]
    l0 = Level(1, 1.0, coef, r0, fx0, fy0, fz0, wt0, d0)
    l1 = Level(2, 0.25, k1, r1, fx1, fy1, fz1, wt1, d1)
    l2 = Level(4, 0.0625, k2, r2, fx2, fy2, fz2, wt2, d2)
    all0, own0, mid0, rim0 = strips(8, 88), strips(16, 80), strips(24, 72), [(8, 16), (72, 16)]
    all1, own1 = strips(8, 56), strips(16, 48)
    all2 = strips(8, 40)

    for c in loads:
        c.wait()
    pl.semaphore_wait(barrier, len(greet))
    coef_in = exchange(0, coef, coef, 3, 16, 3, 64, 3)
    press_in = exchange(5, press, press, 3, 16, 3, 64, 3)
    source_in = exchange(6, source, source, 3, 16, 2, 64, 2)
    coarsen(lambda x, r, n: coef[x, pl.ds(r, n), :], 1, tmp1, k1, (8, 16, lambda j: 2 * j - 13), own0, 16)
    coarsen(lambda x, r, n: k1[x, pl.ds(r, n), :], 2, tmp2, k2, (4, 8, lambda j: 2 * j), own1, 16)
    for p, row in enumerate(pack_rows([k2[4 + i, pl.ds(16, 16), :] for i in range(4)])):
        yk[pl.ds(8 * (4 * parity + gy) + p, 1), :] = row
    k1_in = exchange(1, k1, k1, 8, 8, 8, 32, 8)
    yk_in = gather_near(yk, gather_sem.at[0], gather_sem.at[1])

    l0.inverses((3, 19), own0)
    l0.faces((3, 18), own0)
    l0.diagonal((4, 18), own0)
    l0.sweep(press, source, va0, (4, 18), [(17, 7), *mid0, (72, 7)])
    l0.sweep(va0, source, vb0, (5, 17), mid0)
    residual0 = functools.partial(l0.residual, vb0, source)
    add_planes(residual0, tmp0, (10, 14, lambda j: 2 * j - 13), strips(32, 64))

    arrive(coef_in)
    for planes in ((0, 3), (19, 22)):
        l0.inverses(planes, all0)
    l0.inverses((3, 19), [(8, 8), (80, 8)])
    for planes in ((0, 3), (18, 21)):
        l0.faces(planes, all0)
    l0.faces((3, 18), [(8, 8), (72, 16)])
    for planes in ((1, 4), (18, 21)):
        l0.diagonal(planes, all0)
    l0.diagonal((4, 18), rim0)
    arrive(press_in)
    arrive(source_in)
    for planes in ((1, 4), (18, 21)):
        l0.sweep(press, source, va0, planes, all0)
    l0.sweep(press, source, va0, (4, 18), rim0)
    for planes in ((2, 5), (17, 20)):
        l0.sweep(va0, source, vb0, planes, all0)
    l0.sweep(va0, source, vb0, (5, 17), rim0)
    edge0 = [(16, 16), (64, 16)]
    coarsen(
        residual0, 1, tmp0, g1, (8, 16, lambda j: 2 * j - 13), own0, 16,
        [(8, 10, own0), (10, 14, edge0), (14, 16, own0)],
    )
    even = lane_index((48, LANES)) % 2 == 0

    def pack(q):
        pk1[q, pl.ds(16, 32), :] = jnp.where(even[:32], g1[2 * q, pl.ds(16, 32), :], g1[2 * q + 1, pl.ds(16, 32), :])

    loop(4, 8, pack)
    g1_in = exchange(2, pk1, pk1, 4, 4, 3, 32, 8)
    arrive(yk_in)
    assemble(yk, xk)
    xk_in = gather_x(xk, [6 - 12 * parity, *CHIPS], gather_sem.at[4], gather_sem.at[5])

    arrive(k1_in)
    l1.inverses((0, 24), all1)
    l1.faces((0, 23), all1)
    l1.diagonal((1, 23), all1)
    coarsen(lambda x, r, n: k1[x, pl.ds(r, n), :], 2, tmp2, k2, (0, 12, lambda j: 2 * j), strips(0, 64), 8)
    l2.inverses((0, 12), all2)
    l2.faces((0, 11), all2)
    l2.diagonal((1, 11), all2)

    def keep(x):
        for r, n in own0:
            vs0[x, pl.ds(r, n), :] = vb0[x, pl.ds(r, n), :]

    loop(3, 19, keep)

    arrive(g1_in)

    def unpack(q):
        both = pk1[q, pl.ds(8, 48), :]
        g1[2 * q, pl.ds(8, 48), :] = jnp.where(even, both, roll(both, 1, 1))
        g1[2 * q + 1, pl.ds(8, 48), :] = jnp.where(even, roll(both, -1, 1), both)

    loop(1, 11, unpack)
    v0_in = exchange(3, vb0, vs0, 3, 16, 3, 64, 3)
    l1.first_sweep(g1, va1, (2, 22), all1)
    l1.sweep(va1, g1, vb1, (3, 21), all1)
    coarsen(
        functools.partial(l1.residual, vb1, g1), 2, tmp2, g2, (2, 10, lambda j: 2 * j), all1, 12
    )
    l2.first_sweep(g2, va2, (2, 10), all2)
    l2.sweep(va2, g2, vb2, (3, 9), all2)
    cells = [l2.residual(vb2, g2, 4 + i, 16, 16) for i in range(4)]
    for p, row in enumerate(pack_rows(cells)):
        yg[pl.ds(8 * (4 * parity + gy) + p, 1), :] = row
    yg_in = gather_near(yg, gather_sem.at[2], gather_sem.at[3])
    for x in range(4, 8):
        w2[0, x, pl.ds(16, 16), :] = vb2[x, pl.ds(16, 16), :]
        w2[1, x, pl.ds(16, 16), :] = g2[x, pl.ds(16, 16), :]
    w2_in = exchange(4, w2, w2, 4, 4, 4, 16, 8)
    arrive(xk_in)
    shape = (SLOTS, LANES)
    pack3, pack4 = Packed3(shape), Packed4(shape)
    kk = [xk[pl.ds(i, SLOTS, stride=8), :] for i in range(8)]
    f, d = packed_coefs(pack3, kk, 1.0 / 64)
    for i in range(8):
        for j, value in enumerate((f[0][i], f[1][i], f[2][i], OMEGA * recip(d[i]), d[i])):
            c3[j, i] = value
    l, t = grid2((LANES, LANES))

    def squeeze(values):
        out = None
        for i in range(4):
            y = t // 8 - 4 * i
            choose = jnp.where((l // 32 == y) & ((l % 16) // 2 == t % 8), 0.125, 0.0).astype(BF16)
            part = dot(values[2 * i] + values[2 * i + 1], choose)
            out = part if out is None else out + part
        return out

    f, d = packed_coefs(pack4, [squeeze(kk)], 1.0 / 256)
    weight = OMEGA * recip(d[0])
    faces4 = [weight]
    for axis, prv in enumerate((pack4.x_prev, pack4.y_prev, pack4.z_prev)):
        faces4 += [weight * f[axis][0], weight * prv(f[axis])[0]]
    for j, value in enumerate(faces4):
        c4[j] = value

    arrive(yg_in)
    assemble(yg, xg)
    xg_in = gather_x(xg, CHIPS, gather_sem.at[6], gather_sem.at[7])
    sent(1)
    arrive(xg_in)

    g3 = [xg[pl.ds(i, SLOTS, stride=8), :] for i in range(8)]
    f3 = [[c3[j, i] for i in range(8)] for j in range(3)]
    wt3 = [c3[3, i] for i in range(8)]
    saved = [a * b for a, b in zip(wt3, g3)]
    saved = packed_sweep(pack3, f3, wt3, saved, g3)
    around = pack3.both(f3, saved)
    g4 = squeeze([g3[i] + around[i] - c3[4, i] * saved[i] for i in range(8)])
    f4 = [c4[j] for j in range(7)]
    start = f4[0] * g4

    def coarsest(_, v):
        a = f4[1] * pack4.x_next([v])[0] + f4[2] * pack4.x_prev([v])[0]
        b = f4[3] * pack4.y_next([v])[0] + f4[4] * pack4.y_prev([v])[0]
        c = f4[5] * pack4.z_next([v])[0] + f4[6] * pack4.z_prev([v])[0]
        return ((1.0 - OMEGA) * v + start) + (a + b) + c

    v4 = lax.fori_loop(0, 7, coarsest, start)
    v = []
    for i in range(4):
        y = l // 8 - 4 * i
        spread = jnp.where((t // 32 == y) & ((t % 16) // 2 == l % 8), 1.0, 0.0).astype(BF16)
        part = dot(v4, spread)
        v += [saved[2 * i] + part, saved[2 * i + 1] + part]
    for _ in range(2):
        v = packed_sweep(pack3, f3, wt3, v, g3)
    for i in range(8):
        v3[i] = v[i]

    r, t8 = grid2((8, LANES))
    low = lax.rem(gy + (ngy - 1), ngy)
    high = lax.rem(gy + 1, ngy)
    parts = []
    for j in range(6):
        slot, p = 10 + j // 2, j % 2
        for part, y in ((low, 4), (gy, 0), (gy, 4), (high, 0)):
            rows = [v3[2 * part + p, pl.ds(slot + i, 1), :] for i in range(2)]
            row = jnp.broadcast_to(jnp.where(parity == 1, rows[0], rows[1]), (8, LANES))
            parts.append(jnp.where(t8 // 16 == r // 2 + y, row, 0.0))
    spread = jnp.where(l % 16 == t // 8, 1.0, 0.0).astype(BF16)
    fine = dot(jnp.concatenate(parts, axis=0), spread)
    for j in range(6):
        dup2[j] = fine[32 * j : 32 * j + 32]

    arrive(w2_in)

    def correct2(x):
        va2[x, pl.ds(8, 32), :] = w2[0, x, pl.ds(8, 32), :] + dup2[x // 2]

    loop(0, 12, correct2)
    l2.sweep(va2, w2.at[1], vb2, (1, 11), all2)
    l2.sweep(vb2, w2.at[1], va2, (2, 10), all2)

    def double2(x):
        c = va2[x, pl.ds(12, 24), :]
        dup1[x, pl.ds(8, 24, stride=2), :] = c
        dup1[x, pl.ds(9, 24, stride=2), :] = c

    loop(2, 10, double2)

    def correct1(x):
        for r, n in all1:
            va1[x, pl.ds(r, n), :] = vb1[x, pl.ds(r, n), :] + dup1[x // 2, pl.ds(r, n), :]

    loop(4, 20, correct1)
    l1.sweep(va1, g1, vb1, (5, 19), all1)
    l1.sweep(vb1, g1, va1, (6, 18), all1)

    def double1(x):
        c = va1[x, pl.ds(12, 40), :]
        tmp1[x, pl.ds(8, 40, stride=2), :] = c
        tmp1[x, pl.ds(9, 40, stride=2), :] = c

    loop(6, 18, double1)
    arrive(v0_in)

    def correct0(x):
        for r, n in all0:
            va0[x, pl.ds(r, n), :] = vs0[x, pl.ds(r, n), :] + tmp1[(x + 13) // 2, pl.ds(r, n), :]

    loop(0, 22, correct0)
    l0.sweep(va0, source, vb0, (1, 21), all0)
    l0.sweep(vb0, source, va0, (2, 20), all0)
    v_store = pltpu.make_async_copy(va0.at[pl.ds(3, 16), pl.ds(16, 64), :], v_out, store_sem.at[0])
    v_store.start()

    def final(x):
        for r, n in own0:
            res0[x - 3, pl.ds(r - 16, n), :] = l0.residual(va0, source, x, r, n)

    stores = [v_store]
    for half in range(2):
        loop(3 + 8 * half, 11 + 8 * half, final)
        planes = pl.ds(8 * half, 8)
        stores.append(pltpu.make_async_copy(res0.at[planes], r_out.at[planes], store_sem.at[1 + half]))
        stores[-1].start()
    sent()
    for c in stores:
        c.wait()


def solution(mesh):
    ngx, ngy = mesh.shape["gx"], mesh.shape["gy"]

    def vmem(*shape):
        return pltpu.VMEM(shape, F32)

    n0, n1, n2 = (22, 96, LANES), (24, 64, LANES), (12, 48, LANES)
    scratch = [vmem(3, *n0)] + [vmem(*n0)] * 9 + [vmem(16, 64, LANES)]
    scratch += [vmem(*n1)] * 10 + [vmem(12, 64, LANES)] * 2
    scratch += [vmem(*n2)] * 10 + [vmem(2, *n2), vmem(6, 32, LANES)]
    scratch += [vmem(18, 96, LANES), vmem(12, 64, LANES), vmem(16, 96, LANES)]
    scratch += [vmem(64, LANES)] * 2 + [vmem(8 * SLOTS, LANES)] * 2
    scratch += [vmem(5, 8, SLOTS, LANES), vmem(7, SLOTS, LANES), vmem(8, SLOTS, LANES)]
    dma = pltpu.SemaphoreType.DMA
    scratch += [dma((3,)), dma((3,)), dma((7, 8)), dma((7, 8)), dma((8,))]

    def per_device(pressure, inverse_density, source):
        block = jax.ShapeDtypeStruct(pressure.shape, F32)
        return pl.pallas_call(
            functools.partial(kernel, ngx, ngy),
            out_shape=(block, block),
            in_specs=[pl.BlockSpec(memory_space=pltpu.HBM)] * 3,
            out_specs=[pl.BlockSpec(memory_space=pl.ANY)] * 2,
            scratch_shapes=scratch,
            compiler_params=pltpu.CompilerParams(
                collective_id=0, has_side_effects=True, vmem_limit_bytes=105 * 2**19
            ),
        )(pressure, inverse_density, source)

    spec = P("gx", "gy", None)
    return jax.shard_map(
        per_device, mesh=mesh, in_specs=(spec,) * 3, out_specs=(spec, spec), check_vma=False
    )
```

```python
import functools

import jax
import jax.numpy as jnp
from jax import lax
from jax.experimental import pallas as pl
from jax.experimental.pallas import tpu as pltpu
from jax.sharding import PartitionSpec as P

MESH = pl.DeviceIdType.MESH
F32 = jnp.float32
BF16 = jnp.bfloat16
OMEGA = 0.8
LANES = 128
SIDES = ((-1, 0), (1, 0), (0, -1), (0, 1), (-1, -1), (-1, 1), (1, -1), (1, 1))
SLOTS = 24
CHIPS = [c for d in range(5, 0, -1) for c in (d, -d)]


def recip(x):
    y = pl.reciprocal(x, approx=True)
    return y * (2.0 - x * y)


def roll(x, shift, axis):
    return pltpu.roll(x, shift % x.shape[axis], axis)


def loop(lo, hi, body):
    def step(i, carry):
        body(i)
        return carry

    lax.fori_loop(lo, hi, step, 0, unroll=hi - lo)


def strips(lo, hi, size=16):
    return [(r, min(size, hi - r)) for r in range(lo, hi, size)]


def lane_index(shape):
    return lax.broadcasted_iota(jnp.int32, shape, 1)


def pair_sum_z(x, s):
    first = (lane_index(x.shape) // s) % 2 == 0
    return x + jnp.where(first, roll(x, -s, 1), roll(x, s, 1))


class Level:
    def __init__(self, s, scale, k, r, fx, fy, fz, w, d):
        self.s, self.scale, self.k = s, scale, k
        self.r, self.fx, self.fy, self.fz, self.w, self.d = r, fx, fy, fz, w, d

    def inverses(self, planes, rows):
        def body(x):
            for r, n in rows:
                self.r[x, pl.ds(r, n), :] = (0.5 / self.scale) * recip(self.k[x, pl.ds(r, n), :])

        loop(*planes, body)

    def faces(self, planes, rows):
        def body(x):
            for r, n in rows:
                here = self.r[x, pl.ds(r, n), :]
                self.fx[x, pl.ds(r, n), :] = recip(here + self.r[x + 1, pl.ds(r, n), :])
                self.fy[x, pl.ds(r, n), :] = recip(here + self.r[x, pl.ds(r + 1, n), :])
                self.fz[x, pl.ds(r, n), :] = recip(here + roll(here, -self.s, 1))

        loop(*planes, body)

    def diagonal(self, planes, rows):
        def body(x):
            for r, n in rows:
                fz = self.fz[x, pl.ds(r, n), :]
                d = self.fx[x, pl.ds(r, n), :] + self.fx[x - 1, pl.ds(r, n), :]
                d += self.fy[x, pl.ds(r, n), :] + self.fy[x, pl.ds(r - 1, n), :]
                d += fz + roll(fz, self.s, 1)
                self.d[x, pl.ds(r, n), :] = d
                self.w[x, pl.ds(r, n), :] = OMEGA * recip(d)

        loop(*planes, body)

    def around(self, v, x, r, n):
        here = v[x, pl.ds(r, n), :]
        fz = self.fz[x, pl.ds(r, n), :]
        a = self.fx[x, pl.ds(r, n), :] * v[x + 1, pl.ds(r, n), :]
        a += self.fx[x - 1, pl.ds(r, n), :] * v[x - 1, pl.ds(r, n), :]
        a += self.fy[x, pl.ds(r, n), :] * v[x, pl.ds(r + 1, n), :]
        a += self.fy[x, pl.ds(r - 1, n), :] * v[x, pl.ds(r - 1, n), :]
        a += fz * roll(here, -self.s, 1) + roll(fz * here, self.s, 1)
        return here, a

    def first_sweep(self, g, dst, planes, rows):
        def body(x):
            for r, n in rows:
                dst[x, pl.ds(r, n), :] = self.w[x, pl.ds(r, n), :] * g[x, pl.ds(r, n), :]

        loop(*planes, body)

    def sweep(self, src, g, dst, planes, rows):
        def body(x):
            for r, n in rows:
                here, a = self.around(src, x, r, n)
                w = self.w[x, pl.ds(r, n), :]
                dst[x, pl.ds(r, n), :] = (1.0 - OMEGA) * here + w * (g[x, pl.ds(r, n), :] + a)

        loop(*planes, body)

    def residual(self, v, g, x, r, n):
        here, a = self.around(v, x, r, n)
        return g[x, pl.ds(r, n), :] + a - self.d[x, pl.ds(r, n), :] * here


def add_planes(value, tmp, pairs, rows):
    lo, hi, plane = pairs

    def gather(j):
        x = plane(j)
        for r, n in rows:
            tmp[j, pl.ds(r, n), :] = value(x, r, n) + value(x + 1, r, n)

    loop(lo, hi, gather)


def coarsen(value, s, tmp, dst, pairs, rows, dst_rows, parts=None):
    lo, hi, plane = pairs
    for part_lo, part_hi, part_rows in parts or [(lo, hi, rows)]:
        add_planes(value, tmp, (part_lo, part_hi, plane), part_rows)
    first, count = rows[0][0], sum(n for _, n in rows) // 2

    def squeeze(j):
        even = tmp[j, pl.ds(first, count, stride=2), :]
        odd = tmp[j, pl.ds(first + 1, count, stride=2), :]
        dst[j, pl.ds(dst_rows, count), :] = 0.125 * pair_sum_z(even + odd, s)

    loop(lo, hi, squeeze)


class Packed3:
    def __init__(self, shape):
        lane = lane_index(shape)
        self.y_last, self.y_first = lane >= 112, lane < 16
        self.z_last, self.z_first = lane % 16 == 15, lane % 16 == 0

    def y_next(self, v):
        t = [roll(a, -16, 1) for a in v]
        return [jnp.where(self.y_last, t[(i + 2) % 8], t[i]) for i in range(8)]

    def y_prev(self, v):
        t = [roll(a, 16, 1) for a in v]
        return [jnp.where(self.y_first, t[(i - 2) % 8], t[i]) for i in range(8)]

    def z_next(self, v):
        return [jnp.where(self.z_last, roll(a, 15, 1), roll(a, -1, 1)) for a in v]

    def z_prev(self, v):
        return [jnp.where(self.z_first, roll(a, -15, 1), roll(a, 1, 1)) for a in v]

    def x_next(self, v):
        return [v[i + 1] if i % 2 == 0 else roll(v[i - 1], -1, 0) for i in range(8)]

    def x_prev(self, v):
        return [roll(v[i + 1], 1, 0) if i % 2 == 0 else v[i - 1] for i in range(8)]

    def both(self, f, v):
        out = None
        for axis in range(3):
            nxt = (self.x_next, self.y_next, self.z_next)[axis](v)
            prv = (self.x_prev, self.y_prev, self.z_prev)[axis]([a * b for a, b in zip(f[axis], v)])
            term = [a * b + c for a, b, c in zip(f[axis], nxt, prv)]
            out = term if out is None else [a + b for a, b in zip(out, term)]
        return out


class Packed4(Packed3):
    def __init__(self, shape):
        lane = lane_index(shape)
        self.z_last, self.z_first = lane % 8 == 7, lane % 8 == 0

    def y_next(self, v):
        return [roll(v[0], -8, 1)]

    def y_prev(self, v):
        return [roll(v[0], 8, 1)]

    def z_next(self, v):
        return [jnp.where(self.z_last, roll(v[0], 7, 1), roll(v[0], -1, 1))]

    def z_prev(self, v):
        return [jnp.where(self.z_first, roll(v[0], -7, 1), roll(v[0], 1, 1))]

    def x_next(self, v):
        return [roll(v[0], -1, 0)]

    def x_prev(self, v):
        return [roll(v[0], 1, 0)]


def packed_coefs(pack, k, scale):
    r = [(0.5 / scale) * recip(a) for a in k]
    f = []
    d = None
    for nxt, prv in ((pack.x_next, pack.x_prev), (pack.y_next, pack.y_prev), (pack.z_next, pack.z_prev)):
        face = [recip(a + b) for a, b in zip(r, nxt(r))]
        f.append(face)
        both = [a + b for a, b in zip(face, prv(face))]
        d = both if d is None else [a + b for a, b in zip(d, both)]
    return f, d


def packed_sweep(pack, f, w, v, g):
    return [
        (1.0 - OMEGA) * a + b * (c + e) for a, b, c, e in zip(v, w, g, pack.both(f, v))
    ]


def dot(a, choose):
    out = None
    for _ in range(3):
        part = a.astype(BF16)
        a = a - part.astype(F32)
        term = jnp.dot(part, choose, preferred_element_type=F32)
        out = term if out is None else out + term
    return out


def grid2(shape):
    return lax.broadcasted_iota(jnp.int32, shape, 0), lax.broadcasted_iota(jnp.int32, shape, 1)


def pack_rows(cells):
    l, t = grid2((LANES, LANES))
    choose = jnp.where((l // 8 == t % 16) & (l % 4 == 0), 0.125, 0.0).astype(BF16)
    r, t = grid2((16, LANES))
    keep = r // 2 == t // 16
    rows = []
    for p in range(2):
        u = dot(cells[2 * p] + cells[2 * p + 1], choose)
        rows.append(jnp.sum(jnp.where(keep, u, 0.0), axis=0, keepdims=True))
    return rows


def kernel(
    ngx, ngy, p_hbm, k_hbm, s_hbm, v_out, r_out,
    w0, r0, fx0, fy0, fz0, wt0, d0, va0, vb0, vs0, res0,
    k1, r1, fx1, fy1, fz1, wt1, d1, g1, va1, vb1, dup1, pk1,
    k2, r2, fx2, fy2, fz2, wt2, d2, g2, va2, vb2, w2, pk2, dup2,
    tmp1, tmp2, tmp0, yk, yg, xk, xg, c3, c4, v3,
    load_sem, store_sem, side_s, side_r, gather_sem,
):
    gx, gy = lax.axis_index("gx"), lax.axis_index("gy")
    parity = lax.rem(gx, 2)

    def peer(dx, dy):
        return (lax.rem(gx + (dx + ngx), ngx), lax.rem(gy + (dy + ngy), ngy))

    loads = [
        pltpu.make_async_copy(hbm, w0.at[i, pl.ds(3, 16), pl.ds(16, 64), :], load_sem.at[i])
        for i, hbm in ((1, k_hbm), (0, p_hbm), (2, s_hbm))
    ]
    for c in loads:
        c.start()

    greet = [(2 * c, 0) for c in (6, -6, *CHIPS)] + [(0, 2), (1 - 2 * parity, 2)] + list(SIDES)[::-1]
    barrier = pltpu.get_barrier_semaphore()
    for o in greet:
        pl.semaphore_signal(barrier, inc=1, device_id=peer(*o), device_id_type=MESH)

    waits = []

    def exchange(which, src, dst, x0, nx, hx, ny, hy):
        y0 = 16
        lead = (slice(None),) * (len(src.shape) - 3)
        copies = []
        for i, (dx, dy) in enumerate(SIDES):
            xs, xd, xn = ((x0, x0 + nx, hx), (x0, x0, nx), (x0 + nx - hx, x0 - hx, hx))[dx + 1]
            ys, yd, yn = ((y0, y0 + ny, hy), (y0, y0, ny), (y0 + ny - hy, y0 - hy, hy))[dy + 1]
            c = pltpu.make_async_remote_copy(
                src_ref=src.at[lead + (pl.ds(xs, xn), pl.ds(ys, yn))],
                dst_ref=dst.at[lead + (pl.ds(xd, xn), pl.ds(yd, yn))],
                send_sem=side_s.at[which, i], recv_sem=side_r.at[which, i],
                device_id=peer(dx, dy), device_id_type=MESH,
            )
            c.start()
            copies.append(c)
        waits.extend(copies)
        return copies

    def wait_all(buf, tiles, send, recv):
        every = buf.at[pl.ds(0, 8 * tiles), :]
        c = pltpu.make_async_remote_copy(
            src_ref=every, dst_ref=every, send_sem=send, recv_sem=recv,
            device_id=peer(1, 0), device_id_type=MESH,
        )
        waits.append(c)
        return [c]

    def gather_near(buf, send, recv):
        mine = pl.ds(pl.multiple_of(8 * (4 * parity + gy), 8), 8)
        for dx, dy in ((1, 2), (0, 2), (1, 1), (1, 3), (0, 1), (0, 3), (1, 0)):
            c = pltpu.make_async_remote_copy(
                src_ref=buf.at[mine, :], dst_ref=buf.at[mine, :], send_sem=send, recv_sem=recv,
                device_id=peer(dx * (1 - 2 * parity), dy), device_id_type=MESH,
            )
            c.start()
        return wait_all(buf, 7, send, recv)

    def chip_rows(c):
        return pl.ds(pl.multiple_of(16 * (6 + c - parity), 16), 16)

    def gather_x(buf, chips, send, recv):
        for c in chips:
            copy = pltpu.make_async_remote_copy(
                src_ref=buf.at[chip_rows(0), :], dst_ref=buf.at[chip_rows(-c), :], send_sem=send, recv_sem=recv,
                device_id=peer(2 * c, 0), device_id_type=MESH,
            )
            copy.start()
        return wait_all(buf, 2 * len(chips), send, recv)

    def assemble(near, buf):
        for device in range(2):
            for i in range(4):
                row = pl.multiple_of(8 * (2 * (6 - parity) + device), 8) + 2 * i
                buf[pl.ds(row, 2), :] = near[pl.ds(8 * (4 * device + i), 2), :]

    def arrive(copies):
        for c in copies:
            c.wait_recv()

    def sent(keep=0):
        count = len(waits) - keep
        for c in waits[:count]:
            c.wait_send()
        del waits[:count]

    press, coef, source = w0.at[0], w0.at[1], w0.at[2]
    l0 = Level(1, 1.0, coef, r0, fx0, fy0, fz0, wt0, d0)
    l1 = Level(2, 0.25, k1, r1, fx1, fy1, fz1, wt1, d1)
    l2 = Level(4, 0.0625, k2, r2, fx2, fy2, fz2, wt2, d2)
    all0, own0, mid0, rim0 = strips(8, 88), strips(16, 80), strips(24, 72), [(8, 16), (72, 16)]
    all1, own1 = strips(8, 56), strips(16, 48)
    all2 = strips(8, 40)

    for c in loads:
        c.wait()
    pl.semaphore_wait(barrier, len(greet))
    coef_in = exchange(0, coef, coef, 3, 16, 3, 64, 3)
    press_in = exchange(5, press, press, 3, 16, 3, 64, 3)
    source_in = exchange(6, source, source, 3, 16, 2, 64, 2)
    coarsen(lambda x, r, n: coef[x, pl.ds(r, n), :], 1, tmp1, k1, (8, 16, lambda j: 2 * j - 13), own0, 16)
    coarsen(lambda x, r, n: k1[x, pl.ds(r, n), :], 2, tmp2, k2, (4, 8, lambda j: 2 * j), own1, 16)
    for p, row in enumerate(pack_rows([k2[4 + i, pl.ds(16, 16), :] for i in range(4)])):
        yk[pl.ds(8 * (4 * parity + gy) + p, 1), :] = row
    k1_in = exchange(1, k1, k1, 8, 8, 8, 32, 8)
    yk_in = gather_near(yk, gather_sem.at[0], gather_sem.at[1])

    l0.inverses((3, 19), own0)
    l0.faces((3, 18), own0)
    l0.diagonal((4, 18), own0)
    l0.sweep(press, source, va0, (4, 18), [(17, 7), *mid0, (72, 7)])
    l0.sweep(va0, source, vb0, (5, 17), mid0)
    residual0 = functools.partial(l0.residual, vb0, source)
    add_planes(residual0, tmp0, (10, 14, lambda j: 2 * j - 13), strips(32, 64))

    arrive(coef_in)
    for planes in ((0, 3), (19, 22)):
        l0.inverses(planes, all0)
    l0.inverses((3, 19), [(8, 8), (80, 8)])
    for planes in ((0, 3), (18, 21)):
        l0.faces(planes, all0)
    l0.faces((3, 18), [(8, 8), (72, 16)])
    for planes in ((1, 4), (18, 21)):
        l0.diagonal(planes, all0)
    l0.diagonal((4, 18), rim0)
    arrive(press_in)
    arrive(source_in)
    for planes in ((1, 4), (18, 21)):
        l0.sweep(press, source, va0, planes, all0)
    l0.sweep(press, source, va0, (4, 18), rim0)
    for planes in ((2, 5), (17, 20)):
        l0.sweep(va0, source, vb0, planes, all0)
    l0.sweep(va0, source, vb0, (5, 17), rim0)
    edge0 = [(16, 16), (64, 16)]
    coarsen(
        residual0, 1, tmp0, g1, (8, 16, lambda j: 2 * j - 13), own0, 16,
        [(8, 10, own0), (10, 14, edge0), (14, 16, own0)],
    )
    even = lane_index((48, LANES)) % 2 == 0

    def pack(q):
        pk1[q, pl.ds(16, 32), :] = jnp.where(even[:32], g1[2 * q, pl.ds(16, 32), :], g1[2 * q + 1, pl.ds(16, 32), :])

    loop(4, 8, pack)
    g1_in = exchange(2, pk1, pk1, 4, 4, 3, 32, 8)
    arrive(yk_in)
    assemble(yk, xk)
    xk_in = gather_x(xk, [6 - 12 * parity, *CHIPS], gather_sem.at[4], gather_sem.at[5])

    arrive(k1_in)
    l1.inverses((0, 24), all1)
    l1.faces((0, 23), all1)
    l1.diagonal((1, 23), all1)
    coarsen(lambda x, r, n: k1[x, pl.ds(r, n), :], 2, tmp2, k2, (0, 12, lambda j: 2 * j), strips(0, 64), 8)
    l2.inverses((0, 12), all2)
    l2.faces((0, 11), all2)
    l2.diagonal((1, 11), all2)

    def keep(x):
        for r, n in own0:
            vs0[x, pl.ds(r, n), :] = vb0[x, pl.ds(r, n), :]

    loop(3, 19, keep)

    l1.first_sweep(g1, va1, (8, 16), own1)
    arrive(g1_in)

    def unpack(q, rows):
        for r, n in rows:
            both = pk1[q, pl.ds(r, n), :]
            g1[2 * q, pl.ds(r, n), :] = jnp.where(even[:n], both, roll(both, 1, 1))
            g1[2 * q + 1, pl.ds(r, n), :] = jnp.where(even[:n], roll(both, -1, 1), both)

    rim1 = [(8, 8), (48, 8)]
    loop(1, 4, lambda q: unpack(q, all1))
    loop(8, 11, lambda q: unpack(q, all1))
    loop(4, 8, lambda q: unpack(q, rim1))
    v0_in = exchange(3, vb0, vs0, 3, 16, 3, 64, 3)
    l1.first_sweep(g1, va1, (2, 8), all1)
    l1.first_sweep(g1, va1, (16, 22), all1)
    l1.first_sweep(g1, va1, (8, 16), rim1)
    l1.sweep(va1, g1, vb1, (3, 21), all1)
    coarsen(
        functools.partial(l1.residual, vb1, g1), 2, tmp2, g2, (2, 10, lambda j: 2 * j), all1, 12
    )
    l2.first_sweep(g2, va2, (2, 10), all2)
    l2.sweep(va2, g2, vb2, (3, 9), all2)
    cells = [l2.residual(vb2, g2, 4 + i, 16, 16) for i in range(4)]
    for p, row in enumerate(pack_rows(cells)):
        yg[pl.ds(8 * (4 * parity + gy) + p, 1), :] = row
    yg_in = gather_near(yg, gather_sem.at[2], gather_sem.at[3])
    for x in range(4, 8):
        pk2[x, pl.ds(16, 16), :] = jnp.where(even[:16], vb2[x, pl.ds(16, 16), :], g2[x, pl.ds(16, 16), :])
    w2_in = exchange(4, pk2, pk2, 4, 4, 4, 16, 8)
    arrive(xk_in)
    shape = (SLOTS, LANES)
    pack3, pack4 = Packed3(shape), Packed4(shape)
    kk = [xk[pl.ds(i, SLOTS, stride=8), :] for i in range(8)]
    f, d = packed_coefs(pack3, kk, 1.0 / 64)
    for i in range(8):
        for j, value in enumerate((f[0][i], f[1][i], f[2][i], OMEGA * recip(d[i]), d[i])):
            c3[j, i] = value
    l, t = grid2((LANES, LANES))

    def squeeze(values):
        out = None
        for i in range(4):
            y = t // 8 - 4 * i
            choose = jnp.where((l // 32 == y) & ((l % 16) // 2 == t % 8), 0.125, 0.0).astype(BF16)
            part = dot(values[2 * i] + values[2 * i + 1], choose)
            out = part if out is None else out + part
        return out

    f, d = packed_coefs(pack4, [squeeze(kk)], 1.0 / 256)
    weight = OMEGA * recip(d[0])
    faces4 = [weight]
    for axis, prv in enumerate((pack4.x_prev, pack4.y_prev, pack4.z_prev)):
        faces4 += [weight * f[axis][0], weight * prv(f[axis])[0]]
    for j, value in enumerate(faces4):
        c4[j] = value

    arrive(yg_in)
    assemble(yg, xg)
    xg_in = gather_x(xg, CHIPS, gather_sem.at[6], gather_sem.at[7])
    sent(1)
    arrive(xg_in)

    g3 = [xg[pl.ds(i, SLOTS, stride=8), :] for i in range(8)]
    f3 = [[c3[j, i] for i in range(8)] for j in range(3)]
    wt3 = [c3[3, i] for i in range(8)]
    saved = [a * b for a, b in zip(wt3, g3)]
    saved = packed_sweep(pack3, f3, wt3, saved, g3)
    around = pack3.both(f3, saved)
    g4 = squeeze([g3[i] + around[i] - c3[4, i] * saved[i] for i in range(8)])
    f4 = [c4[j] for j in range(7)]
    start = f4[0] * g4

    def coarsest(_, v):
        a = f4[1] * pack4.x_next([v])[0] + f4[2] * pack4.x_prev([v])[0]
        b = f4[3] * pack4.y_next([v])[0] + f4[4] * pack4.y_prev([v])[0]
        c = f4[5] * pack4.z_next([v])[0] + f4[6] * pack4.z_prev([v])[0]
        return ((1.0 - OMEGA) * v + start) + (a + b) + c

    v4 = lax.fori_loop(0, 7, coarsest, start, unroll=7)
    v = []
    for i in range(4):
        y = l // 8 - 4 * i
        spread = jnp.where((t // 32 == y) & ((t % 16) // 2 == l % 8), 1.0, 0.0).astype(BF16)
        part = dot(v4, spread)
        v += [saved[2 * i] + part, saved[2 * i + 1] + part]
    for _ in range(2):
        v = packed_sweep(pack3, f3, wt3, v, g3)
    for i in range(8):
        v3[i] = v[i]

    r, t8 = grid2((8, LANES))
    low = lax.rem(gy + (ngy - 1), ngy)
    high = lax.rem(gy + 1, ngy)
    parts = []
    for j in range(6):
        slot, p = 10 + j // 2, j % 2
        for part, y in ((low, 4), (gy, 0), (gy, 4), (high, 0)):
            rows = [v3[2 * part + p, pl.ds(slot + i, 1), :] for i in range(2)]
            row = jnp.broadcast_to(jnp.where(parity == 1, rows[0], rows[1]), (8, LANES))
            parts.append(jnp.where(t8 // 16 == r // 2 + y, row, 0.0))
    spread = jnp.where(l % 16 == t // 8, 1.0, 0.0).astype(BF16)
    fine = dot(jnp.concatenate(parts, axis=0), spread)
    for j in range(6):
        dup2[j] = fine[32 * j : 32 * j + 32]

    arrive(w2_in)

    def correct2(x):
        both = pk2[x, pl.ds(8, 32), :]
        va2[x, pl.ds(8, 32), :] = jnp.where(even[:32], both, roll(both, 1, 1)) + dup2[x // 2]
        w2[x, pl.ds(8, 32), :] = jnp.where(even[:32], roll(both, -1, 1), both)

    loop(0, 12, correct2)
    l2.sweep(va2, w2, vb2, (1, 11), all2)
    l2.sweep(vb2, w2, va2, (2, 10), all2)

    def double2(x):
        c = va2[x, pl.ds(12, 24), :]
        dup1[x, pl.ds(8, 24, stride=2), :] = c
        dup1[x, pl.ds(9, 24, stride=2), :] = c

    loop(2, 10, double2)

    def correct1(x):
        for r, n in all1:
            va1[x, pl.ds(r, n), :] = vb1[x, pl.ds(r, n), :] + dup1[x // 2, pl.ds(r, n), :]

    loop(4, 20, correct1)
    l1.sweep(va1, g1, vb1, (5, 19), all1)
    l1.sweep(vb1, g1, va1, (6, 18), all1)

    def double1(x):
        c = va1[x, pl.ds(12, 40), :]
        tmp1[x, pl.ds(8, 40, stride=2), :] = c
        tmp1[x, pl.ds(9, 40, stride=2), :] = c

    loop(6, 18, double1)
    arrive(v0_in)

    def correct0(x):
        for r, n in all0:
            va0[x, pl.ds(r, n), :] = vs0[x, pl.ds(r, n), :] + tmp1[(x + 13) // 2, pl.ds(r, n), :]

    loop(0, 22, correct0)
    l0.sweep(va0, source, vb0, (1, 21), all0)
    l0.sweep(vb0, source, va0, (2, 20), all0)
    v_store = pltpu.make_async_copy(va0.at[pl.ds(3, 16), pl.ds(16, 64), :], v_out, store_sem.at[0])
    v_store.start()

    def final(x):
        for r, n in own0:
            res0[x - 3, pl.ds(r - 16, n), :] = l0.residual(va0, source, x, r, n)

    stores = [v_store]
    for half in range(2):
        loop(3 + 8 * half, 11 + 8 * half, final)
        planes = pl.ds(8 * half, 8)
        stores.append(pltpu.make_async_copy(res0.at[planes], r_out.at[planes], store_sem.at[1 + half]))
        stores[-1].start()
    sent()
    for c in stores:
        c.wait()


def solution(mesh):
    ngx, ngy = mesh.shape["gx"], mesh.shape["gy"]

    def vmem(*shape):
        return pltpu.VMEM(shape, F32)

    n0, n1, n2 = (22, 96, LANES), (24, 64, LANES), (12, 48, LANES)
    scratch = [vmem(3, *n0)] + [vmem(*n0)] * 9 + [vmem(16, 64, LANES)]
    scratch += [vmem(*n1)] * 10 + [vmem(12, 64, LANES)] * 2
    scratch += [vmem(*n2)] * 10 + [vmem(*n2), vmem(*n2), vmem(6, 32, LANES)]
    scratch += [vmem(18, 96, LANES), vmem(12, 64, LANES), vmem(16, 96, LANES)]
    scratch += [vmem(64, LANES)] * 2 + [vmem(8 * SLOTS, LANES)] * 2
    scratch += [vmem(5, 8, SLOTS, LANES), vmem(7, SLOTS, LANES), vmem(8, SLOTS, LANES)]
    dma = pltpu.SemaphoreType.DMA
    scratch += [dma((3,)), dma((3,)), dma((7, 8)), dma((7, 8)), dma((8,))]

    def per_device(pressure, inverse_density, source):
        block = jax.ShapeDtypeStruct(pressure.shape, F32)
        return pl.pallas_call(
            functools.partial(kernel, ngx, ngy),
            out_shape=(block, block),
            in_specs=[pl.BlockSpec(memory_space=pltpu.HBM)] * 3,
            out_specs=[pl.BlockSpec(memory_space=pl.ANY)] * 2,
            scratch_shapes=scratch,
            compiler_params=pltpu.CompilerParams(
                collective_id=0, has_side_effects=True, vmem_limit_bytes=105 * 2**19
            ),
        )(pressure, inverse_density, source)

    spec = P("gx", "gy", None)
    return jax.shard_map(
        per_device, mesh=mesh, in_specs=(spec,) * 3, out_specs=(spec, spec), check_vma=False
    )
```
